256 devices in a mesh: pipe: 16 (over y, x), dp: 16 (over z, core).
Axes of the slice: x: 4, y: 4, z: 8, core: 2. Of those that a mesh axis runs over, the one named last changes fastest.
Arguments:
- embedded: bfloat16 [2048, 1024], P('dp'), may hold values from -6 to 6
- targets: bfloat16 [2048, 1024], P('dp'), may hold values from -6 to 6
- w_up: bfloat16 [16, 1024, 2048], P('pipe'), may hold values from -0.1875 to 0.1875
- w_down: bfloat16 [16, 2048, 1024], P('pipe'), may hold values from -0.125 to 0.125
- probe_up: bfloat16 [16, 1024, 2048], P('pipe', 'dp'), may hold values from -5 to 5
- probe_down: bfloat16 [16, 1024, 2048], P('pipe', 'dp'), may hold values from -5 to 5
Outputs:
- curv_up: float32 [16, 1024, 2048], P('pipe', 'dp')
- curv_down: float32 [16, 1024, 2048], P('pipe', 'dp')
The draws below stay inside these ranges and needn't reach their ends.
All inputs are finite; a program needn't handle non-finite values.
Results may differ from the reference program's by a relative error of at most 0.022.
Values may be sent and summed in bfloat16 or wider, within the bound.
No kernel may reach another device: no remote copies, remote signals or barrier semaphores. Data moves between devices by JAX's collectives and lax.ppermute only.
A program may use at most 128 MiB of HBM per device.

```python
import jax
import jax.numpy as jnp
from jax import lax

D = 1024
FF = 2048
LAYERS = 16
TOKENS = 2048


def spiked(entries, rng, source, target, shards_of, factor):
    owner, partner = [(jnp.arange(entries.shape[position]) // (entries.shape[position] // shards_of)).reshape([-1 if axis == position else 1 for axis in range(entries.ndim)]) for position in (source, target)]
    chosen = jax.random.permutation(rng, shards_of)[partner]
    strong = (owner == chosen) | (owner == (partner + shards_of // 2) % shards_of)
    return jnp.where(strong, factor * entries, entries)


def block_levels(rng, extent, split, smallest, largest):
    loudness = 1.0
    for axis_at, parts in split:
        draws = jax.random.uniform(jax.random.fold_in(jax.random.fold_in(rng, 6), axis_at), (parts,), jnp.float32, smallest / len(split), largest / len(split))
        loudness = loudness * jnp.repeat(jnp.exp(draws), extent[axis_at] // parts).reshape((-1,) + (1,) * (len(extent) - 1 - axis_at))
    return loudness


def gaussian(key, extent, scale, reach, split=(), kind=jnp.bfloat16):
    result = scale * jax.random.normal(key, extent, jnp.float32)
    if split:
        result = result * block_levels(key, extent, split, -0.22, 0.18)
    return jnp.clip(result, -reach, reach).astype(kind)


def bell_draw_with(key, extent, scale, most, cuts, heavy, held_as=jnp.bfloat16):
    result = scale * jax.random.normal(key, extent, jnp.float32)
    if cuts:
        result = result * block_levels(key, extent, cuts, -0.22, 0.18)
    return jnp.clip(spiked(result, jax.random.fold_in(key, 3), *heavy), -most, most).astype(held_as)


def setup_inputs(seed: int = 0) -> dict:
    streams_of = jax.random.split(jax.random.key(seed), 7)
    return {
        "embedded": bell_draw_with(streams_of[0], (TOKENS, D), 1.0, 6.0, ((0, 16),), (0, 1, 16, 2.0)),
        "targets": gaussian(streams_of[1], (TOKENS, D), 1.0, 6.0, ((0, 16),)),
        "w_up": gaussian(streams_of[2], (LAYERS, D, FF), D ** -0.5, 0.1875, ((0, 16),)),
        "w_down": gaussian(streams_of[3], (LAYERS, FF, D), FF ** -0.5, 0.125, ((0, 16),)),
        "probe_up": gaussian(streams_of[4], (LAYERS, D, FF), 1.0, 5.0, ((0, 16), (1, 16))),
        "probe_down": gaussian(streams_of[5], (LAYERS, D, FF), 1.0, 5.0, ((0, 16), (1, 16))),
    }


epsilon = 1e-05
half_root = 0.7071067811865476
density_scale = 0.3989422804014327

def gelu_terms(values):
    normal_cdf = 0.5 * (1.0 + jax.scipy.special.erf(values * half_root))
    density = density_scale * jnp.exp(-0.5 * values * values)
    return (values * normal_cdf, normal_cdf + values * density, density * (2.0 - values * values))

def normalize(stream):
    centre = stream - lax.optimization_barrier(jnp.mean(stream, axis=-1, keepdims=True))
    spread = lax.optimization_barrier(jnp.mean(centre * centre, axis=-1, keepdims=True))
    return centre * lax.rsqrt(spread + epsilon)

def normalize_back(stream, cotangent):
    unused, pullback = jax.vjp(normalize, stream)
    return pullback(cotangent)[0]

def contract_last(left, right):
    return lax.dot_general(left, right, (((1,), (1,)), ((), ())), preferred_element_type=jnp.float32)

def contract_first(left, right):
    return lax.dot_general(left, right, (((0,), (0,)), ((), ())), preferred_element_type=jnp.float32)

def layer_forward(stream, tangent, w_one, w_two, probe_one, probe_two):
    stream_f = stream.astype(jnp.float32)
    tangent_f = tangent.astype(jnp.float32)
    normed, normed_tan = jax.jvp(normalize, (stream_f,), (tangent_f,))
    normed_b = normed.astype(jnp.bfloat16)
    normed_tb = normed_tan.astype(jnp.bfloat16)
    pre_act = jnp.dot(normed_b, w_one, preferred_element_type=jnp.float32)
    pre_tan = jnp.dot(normed_tb, w_one, preferred_element_type=jnp.float32) + jnp.dot(normed_b, probe_one, preferred_element_type=jnp.float32)
    active, slope, unused = gelu_terms(pre_act)
    active_b = active.astype(jnp.bfloat16)
    active_tb = (slope * pre_tan).astype(jnp.bfloat16)
    branch = jnp.dot(active_b, w_two, preferred_element_type=jnp.float32)
    branch_tan = jnp.dot(active_tb, w_two, preferred_element_type=jnp.float32) + contract_last(active_b, probe_two)
    next_stream = (stream_f + branch).astype(jnp.bfloat16)
    next_tan = (tangent_f + branch_tan).astype(jnp.bfloat16)
    return (next_stream, next_tan, (normed_b, normed_tb, pre_act, pre_tan, active_b, active_tb))

def layer_backward(cotan, cotan_tan, stream, tangent, pre_act, pre_tan, w_one, w_two, probe_one, probe_two):
    grad_act = contract_last(cotan, w_two)
    grad_act_tan = contract_last(cotan_tan, w_two) + jnp.dot(cotan, probe_two, preferred_element_type=jnp.float32)
    unused, slope, curve = gelu_terms(pre_act)
    grad_pre = (grad_act * slope).astype(jnp.bfloat16)
    grad_pre_tan = (grad_act_tan * slope + grad_act * curve * pre_tan).astype(jnp.bfloat16)
    grad_norm = contract_last(grad_pre, w_one)
    grad_norm_tan = contract_last(grad_pre_tan, w_one) + contract_last(grad_pre, probe_one)
    stream_f = stream.astype(jnp.float32)
    tangent_f = tangent.astype(jnp.float32)
    back, back_tan = jax.jvp(normalize_back, (stream_f, grad_norm), (tangent_f, grad_norm_tan))
    previous = (cotan.astype(jnp.float32) + back).astype(jnp.bfloat16)
    previous_tan = (cotan_tan.astype(jnp.float32) + back_tan).astype(jnp.bfloat16)
    return (previous, previous_tan, grad_pre, grad_pre_tan)

def reference(embedded, targets, w_up, w_down, probe_up, probe_down):
    stream = embedded
    tangent = jnp.zeros_like(embedded)
    saved = []
    for layer_index in range(LAYERS):
        next_stream, next_tan, kept = layer_forward(stream, tangent, w_up[layer_index], w_down[layer_index], probe_up[layer_index], probe_down[layer_index])
        saved.append((stream, tangent) + kept)
        stream, tangent = (next_stream, next_tan)
    loss_scale = 1.0 / TOKENS
    cotan = ((stream.astype(jnp.float32) - targets.astype(jnp.float32)) * loss_scale).astype(jnp.bfloat16)
    cotan_tan = (tangent.astype(jnp.float32) * loss_scale).astype(jnp.bfloat16)
    ups = []
    downs = []
    for layer_index in reversed(range(LAYERS)):
        stream_in, tangent_in, normed_b, normed_tb, pre_act, pre_tan, active_b, active_tb = saved[layer_index]
        previous, previous_tan, grad_pre, grad_pre_tan = layer_backward(cotan, cotan_tan, stream_in, tangent_in, pre_act, pre_tan, w_up[layer_index], w_down[layer_index], probe_up[layer_index], probe_down[layer_index])
        term_one = contract_first(jnp.concatenate((normed_b, normed_tb), axis=0), jnp.concatenate((grad_pre_tan, grad_pre), axis=0))
        term_two = contract_first(jnp.concatenate((cotan_tan, cotan), axis=0), jnp.concatenate((active_b, active_tb), axis=0))
        ups.append(probe_up[layer_index].astype(jnp.float32) * term_one)
        downs.append(probe_down[layer_index].astype(jnp.float32) * term_two)
        cotan, cotan_tan = (previous, previous_tan)
    curv_up = jnp.stack(ups[::-1])
    curv_down = jnp.stack(downs[::-1])
    return (curv_up, curv_down)
```

```python
import functools

import jax
import jax.numpy as jnp
from jax import lax
from jax.experimental import pallas as pl
from jax.experimental.pallas import tpu as pltpu
from jax.sharding import PartitionSpec as P

PIECES = 4
LAG = 12
CHUNK = 512

epsilon = 1e-05
half_root = 0.7071067811865476
density_scale = 0.3989422804014327

f32 = jnp.float32
bf16 = jnp.bfloat16

X, TX, G, TG = range(4)
A, TA, PR, TP = range(4)
XH, TXF, QN, BN, PU, AV = range(6)
SLOPE, CURVE, TY, XU, CC, GV = range(6)
INV, RR, M1 = range(3)

IN_VMEM = pl.BlockSpec(memory_space=pltpu.VMEM)
ANYWHERE = pl.BlockSpec(memory_space=pl.ANY)


def vmem(array):
    return pltpu.with_memory_space_constraint(array, pltpu.VMEM)


def hbm(array):
    return pltpu.with_memory_space_constraint(array, pltpu.HBM)


def dot(left, right):
    return jnp.dot(left, right, preferred_element_type=f32)


def dot_last(left, right):
    return lax.dot_general(left, right, (((1,), (1,)), ((), ())), preferred_element_type=f32)


def dot_first(left, right):
    return lax.dot_general(left, right, (((0,), (0,)), ((), ())), preferred_element_type=f32)


def mean(values):
    return jnp.mean(values, axis=-1, keepdims=True)


def gelu_terms(values):
    normal_cdf = 0.5 * (1.0 + lax.erf(values * half_root))
    density = density_scale * jnp.exp(-0.5 * values * values)
    return (values * normal_cdf, normal_cdf + values * density, density * (2.0 - values * values))


def load(arrays):
    count = len(arrays)

    def kernel(*refs):
        sources, targets, sems = refs[:count], refs[count : 2 * count], refs[2 * count]
        copies = [
            pltpu.make_async_copy(source, target, sems.at[i])
            for i, (source, target) in enumerate(zip(sources, targets))
        ]
        for copy in copies:
            copy.start()
        for copy in copies:
            copy.wait()

    return pl.pallas_call(
        kernel,
        out_shape=tuple(pltpu.VMEM(a.shape, a.dtype) for a in arrays),
        in_specs=[ANYWHERE] * count,
        out_specs=(IN_VMEM,) * count,
        scratch_shapes=[pltpu.SemaphoreType.DMA((count,))],
        compiler_params=pltpu.CompilerParams(vmem_limit_bytes=1 << 20),
        name="load",
    )(*[hbm(a) for a in arrays])


def blank(shapes):
    def kernel(*refs):
        refs[-1][...] = jnp.zeros(refs[-1].shape, refs[-1].dtype)

    return pl.pallas_call(
        kernel,
        out_shape=tuple(pltpu.VMEM(shape, kind) for shape, kind in shapes),
        out_specs=(IN_VMEM,) * len(shapes),
        compiler_params=pltpu.CompilerParams(vmem_limit_bytes=1 << 20),
        name="blank",
    )()


class Plan:
    def __init__(self, layers, pieces, lag):
        self.layers, self.pieces, self.lag = layers, pieces, lag
        self.ticks = 2 * layers + lag + pieces - 1

    def stages(self, first, step):
        found = [first - step * m for m in range(self.pieces)]
        return [s for s in found if 0 <= s < self.layers]

    def forward(self, t):
        return self.stages(t, 1)

    def forward_tan(self, t):
        return self.stages(t - self.lag, 1)

    def backward(self, t):
        return self.stages(2 * self.layers - 1 - t, -1)

    def backward_tan(self, t):
        return self.stages(2 * self.layers - 1 - t + self.lag, -1)

    def ready_forward(self, t):
        return 0 <= t - (self.lag - 1) < self.layers

    def ready_backward(self, t):
        return 0 <= 2 * self.layers - 2 + self.lag - t < self.layers

    def edges(self, t):
        up = [(s, s + 1) for s in self.forward(t) + self.forward_tan(t) if s + 1 < self.layers]
        down = [(s, s - 1) for s in self.backward(t) + self.backward_tan(t) if s > 0]
        return up, down


def disjoint(edges):
    sources, targets = [e[0] for e in edges], [e[1] for e in edges]
    return len(set(sources)) == len(sources) and len(set(targets)) == len(targets)


def tick_kernel(plan, t, split_in, split_out, with_probes, loss_scale, rows, width, hidden, *refs):
    refs = list(refs)
    state_in = refs[:5]
    del state_in
    refs = refs[5:]
    w_up, w_down, source, goal = refs[:4]
    refs = refs[4:]
    if with_probes:
        u_up, u_down = refs[:2]
        refs = refs[2:]
    got_up = refs.pop(0)
    got_down = refs.pop(0) if split_in else got_up
    sb_d, sb_f, sf_d, sf_f, sf_n = refs[:5]
    refs = refs[5:]
    put_up = refs.pop(0)
    put_down = refs.pop(0) if split_out else put_up

    layers, pieces, lag = plan.layers, plan.pieces, plan.lag
    stage = lax.axis_index("pipe")
    at_first, at_last = stage == 0, stage == layers - 1
    chunks = [slice(c, c + CHUNK) for c in range(0, hidden, CHUNK)]
    lanes = (rows, 128)

    def when_due(piece, work):
        @pl.when((piece >= 0) & (piece < pieces))
        def _():
            work(pl.ds(pl.multiple_of(jnp.clip(piece, 0, pieces - 1) * rows, rows), rows))

    def spread(value):
        return jnp.broadcast_to(value, lanes)

    def narrow(slot, at):
        return sf_n[slot, at, :][:, :1]

    def forward(at):
        stream = jnp.where(at_first, source[at, :], got_up[...]).astype(f32)
        centre = stream - mean(stream)
        inverse = lax.rsqrt(mean(centre * centre) + epsilon)
        normed = centre * inverse
        sf_d[XH, at, :] = normed
        sf_n[INV, at, :] = spread(inverse)
        normed_b = normed.astype(bf16)
        sb_d[X, at, :] = normed_b
        total = stream
        for c in chunks:
            active, slope, curve = gelu_terms(dot(normed_b, w_up[:, c]))
            active_b = active.astype(bf16)
            sb_f[A, at, c] = active_b
            sf_f[SLOPE, at, c] = slope
            sf_f[CURVE, at, c] = curve
            total = total + dot(active_b, w_down[c, :])
        result = total.astype(bf16)

        @pl.when(jnp.logical_not(at_last))
        def _():
            put_up[...] = result

        @pl.when(at_last)
        def _():
            gap = result.astype(f32) - goal[at, :].astype(f32)
            sb_d[G, at, :] = (gap * loss_scale).astype(bf16)

    def ready_forward():
        for c in chunks:
            sf_f[XU, :, c] = dot(sb_d[X], u_up[:, c])
        for c in [slice(c, c + CHUNK) for c in range(0, width, CHUNK)]:
            sf_d[AV, :, c] = dot_last(sb_f[A], u_down[c, :])

    def forward_tan(at):
        tangent = got_up[...].astype(f32)
        tangent = jnp.where(at_first, jnp.zeros_like(tangent), tangent)
        normed = sf_d[XH, at, :]
        inverse = narrow(INV, at)
        centre = tangent - mean(tangent)
        ratio = mean(normed * centre)
        normed_t = inverse * (centre - normed * ratio)
        sf_d[TXF, at, :] = normed_t
        sf_n[RR, at, :] = spread(-inverse * ratio)
        normed_tb = normed_t.astype(bf16)
        sb_d[TX, at, :] = normed_tb
        total = tangent + sf_d[AV, at, :]
        for c in chunks:
            pre_tan = dot(normed_tb, w_up[:, c]) + sf_f[XU, at, c]
            sf_f[TY, at, c] = pre_tan
            active_tb = (sf_f[SLOPE, at, c] * pre_tan).astype(bf16)
            sb_f[TA, at, c] = active_tb
            total = total + dot(active_tb, w_down[c, :])
        result = total.astype(bf16)

        @pl.when(jnp.logical_not(at_last))
        def _():
            put_up[...] = result

        @pl.when(at_last)
        def _():
            sb_d[TG, at, :] = (result.astype(f32) * loss_scale).astype(bf16)

    def backward(at):
        cotan = jnp.where(at_last, sb_d[G, at, :], got_down[...])
        sb_d[G, at, :] = cotan
        grad = jnp.zeros((rows, width), f32)
        for c in chunks:
            grad_act = dot_last(cotan, w_down[c, :])
            sf_f[CC, at, c] = grad_act * sf_f[CURVE, at, c]
            grad_pre = (grad_act * sf_f[SLOPE, at, c]).astype(bf16)
            sb_f[PR, at, c] = grad_pre
            grad = grad + dot_last(grad_pre, w_up[:, c])
        sf_d[QN, at, :] = grad
        normed = sf_d[XH, at, :]
        along = mean(grad * normed)
        sf_n[M1, at, :] = spread(along)
        back = narrow(INV, at) * (grad - mean(grad) - normed * along)
        sf_d[BN, at, :] = back
        result = (cotan.astype(f32) + back).astype(bf16)

        @pl.when(jnp.logical_not(at_first))
        def _():
            put_down[...] = result

    def ready_backward():
        for c in chunks:
            sf_f[GV, :, c] = dot(sb_d[G], u_down[:, c])
        for c in [slice(c, c + CHUNK) for c in range(0, width, CHUNK)]:
            sf_d[PU, :, c] = dot_last(sb_f[PR], u_up[c, :])

    def backward_tan(at):
        cotan_t = jnp.where(at_last, sb_d[TG, at, :], got_down[...])
        sb_d[TG, at, :] = cotan_t
        grad_t = sf_d[PU, at, :]
        for c in chunks:
            grad_act_t = dot_last(cotan_t, w_down[c, :]) + sf_f[GV, at, c]
            grad_pre_t = grad_act_t * sf_f[SLOPE, at, c] + sf_f[CC, at, c] * sf_f[TY, at, c]
            grad_pre_tb = grad_pre_t.astype(bf16)
            sb_f[TP, at, c] = grad_pre_tb
            grad_t = grad_t + dot_last(grad_pre_tb, w_up[:, c])
        normed, normed_t, inverse = sf_d[XH, at, :], sf_d[TXF, at, :], narrow(INV, at)
        along_t = mean(grad_t * normed + sf_d[QN, at, :] * normed_t)
        inner = grad_t - mean(grad_t) - normed_t * narrow(M1, at) - normed * along_t
        back_t = narrow(RR, at) * sf_d[BN, at, :] + inverse * inner
        result = (cotan_t.astype(f32) + back_t).astype(bf16)

        @pl.when(jnp.logical_not(at_first))
        def _():
            put_down[...] = result

    if plan.backward_tan(t):
        when_due(t - lag - (2 * layers - 1 - stage), backward_tan)
    if plan.forward_tan(t):
        when_due(t - lag - stage, forward_tan)
    if plan.backward(t):
        when_due(t - (2 * layers - 1 - stage), backward)
    if plan.forward(t):
        when_due(t - stage, forward)
    if plan.ready_forward(t):
        pl.when(stage == t - (lag - 1))(ready_forward)
    if plan.ready_backward(t):
        pl.when(stage == 2 * layers - 2 + lag - t)(ready_backward)


def curvature_kernel(sb_d, sb_f, out, hold, sems):
    width, hidden = sb_d.shape[2], sb_f.shape[2]
    step = hold.shape[1]
    copies = []
    for i in range(width // step):
        at = slice(i * step, (i + 1) * step)
        if i >= 2:
            copies[i - 2].wait()
        left = jnp.concatenate((sb_d[X, :, at], sb_d[TX, :, at]), axis=0)
        right = jnp.concatenate((sb_f[TP], sb_f[PR]), axis=0)
        hold[i % 2, :, :hidden] = dot_first(left, right).astype(bf16)
        left = jnp.concatenate((sb_d[TG, :, at], sb_d[G, :, at]), axis=0)
        right = jnp.concatenate((sb_f[A], sb_f[TA]), axis=0)
        hold[i % 2, :, hidden:] = dot_first(left, right).astype(bf16)
        copy = pltpu.make_async_copy(hold.at[i % 2], out.at[at, :], sems.at[i % 2])
        copy.start()
        copies.append(copy)
    for copy in copies[-2:]:
        copy.wait()


def curvature(sb_d, sb_f):
    width, hidden = sb_d.shape[2], sb_f.shape[2]
    step = 128
    return pl.pallas_call(
        curvature_kernel,
        out_shape=jax.ShapeDtypeStruct((width, 2 * hidden), bf16),
        in_specs=[IN_VMEM, IN_VMEM],
        out_specs=ANYWHERE,
        scratch_shapes=[
            pltpu.VMEM((2, step, 2 * hidden), bf16),
            pltpu.SemaphoreType.DMA((2,)),
        ],
        compiler_params=pltpu.CompilerParams(vmem_limit_bytes=16 << 20),
        name="curvature",
    )(vmem(sb_d), vmem(sb_f))


def on_device(embedded, targets, w_up, w_down, probe_up, probe_down):
    layers = lax.axis_size("pipe")
    groups = lax.axis_size("dp")
    tokens, width = embedded.shape
    hidden = w_up.shape[2]
    rows = tokens // PIECES
    loss_scale = 1.0 / (tokens * groups)
    plan = Plan(layers, PIECES, LAG)

    gathered = [
        lax.all_gather(probe[0], "dp", axis=0, tiled=True) for probe in (probe_up, probe_down)
    ]
    held = load((w_up[0], w_down[0], embedded, targets))
    *state, nothing = blank(
        (
            ((4, tokens, width), bf16),
            ((4, tokens, hidden), bf16),
            ((6, tokens, width), f32),
            ((6, tokens, hidden), f32),
            ((3, tokens, 128), f32),
            ((rows, width), bf16),
        )
    )
    probes = None
    got = (nothing,)
    packet = pltpu.VMEM((rows, width), bf16)
    for t in range(plan.ticks):
        if t == LAG - 1:
            probes = load(gathered)
        up, down = plan.edges(t)
        split_out = not disjoint(up + down)
        with_probes = plan.ready_forward(t) or plan.ready_backward(t)
        operands = list(state) + list(held) + (list(probes) if with_probes else []) + list(got)
        results = 2 if split_out else 1
        outs = pl.pallas_call(
            functools.partial(
                tick_kernel, plan, t, len(got) == 2, split_out, with_probes, loss_scale, rows, width, hidden
            ),
            out_shape=tuple(pltpu.VMEM(s.shape, s.dtype) for s in state) + (packet,) * results,
            in_specs=[IN_VMEM] * len(operands),
            out_specs=(IN_VMEM,) * (5 + results),
            input_output_aliases={i: i for i in range(5)},
            compiler_params=pltpu.CompilerParams(vmem_limit_bytes=8 << 20),
            cost_estimate=pl.CostEstimate(flops=1 << 28, bytes_accessed=1 << 23, transcendentals=0),
            name="tick",
        )(*[vmem(o) for o in operands])
        state, sent = outs[:5], outs[5:]
        if split_out:
            got = (lax.ppermute(sent[0], "pipe", up), lax.ppermute(sent[1], "pipe", down))
        elif up + down:
            got = (lax.ppermute(sent[0], "pipe", up + down),)

    sums = curvature(state[0], state[1])
    summed = lax.psum_scatter(sums, "dp", scatter_dimension=0, tiled=True).astype(f32)
    curv_up = probe_up[0].astype(f32) * summed[:, :hidden]
    curv_down = probe_down[0].astype(f32) * summed[:, hidden:]
    return (curv_up[None], curv_down[None])


def solution(mesh):
    in_specs = (
        P("dp", None),
        P("dp", None),
        P("pipe", None, None),
        P("pipe", None, None),
        P("pipe", "dp", None),
        P("pipe", "dp", None),
    )
    out_specs = (P("pipe", "dp", None), P("pipe", "dp", None))
    return jax.shard_map(
        on_device, mesh=mesh, in_specs=in_specs, out_specs=out_specs, check_vma=False
    )
```

```python
import functools

import jax
import jax.numpy as jnp
from jax import lax
from jax.experimental import pallas as pl
from jax.experimental.pallas import tpu as pltpu
from jax.sharding import PartitionSpec as P

PIECES = 4
LAG = 7
CHUNK = 512

epsilon = 1e-05
half_root = 0.7071067811865476
density_scale = 0.3989422804014327

f32 = jnp.float32
bf16 = jnp.bfloat16

X, TX, G, TG = range(4)
A, TA, PR, TP = range(4)
XH, TXF, QN, BN, PU, AV = range(6)
SLOPE, CURVE, TY, XU, CC, GV = range(6)
INV, RR, M1 = range(3)

IN_VMEM = pl.BlockSpec(memory_space=pltpu.VMEM)
ANYWHERE = pl.BlockSpec(memory_space=pl.ANY)


def vmem(array):
    return pltpu.with_memory_space_constraint(array, pltpu.VMEM)


def hbm(array):
    return pltpu.with_memory_space_constraint(array, pltpu.HBM)


def dot(left, right):
    return jnp.dot(left, right, preferred_element_type=f32)


def dot_last(left, right):
    return lax.dot_general(left, right, (((1,), (1,)), ((), ())), preferred_element_type=f32)


def dot_first(left, right):
    return lax.dot_general(left, right, (((0,), (0,)), ((), ())), preferred_element_type=f32)


def mean(values):
    return jnp.mean(values, axis=-1, keepdims=True)


def gelu_terms(values):
    normal_cdf = 0.5 * (1.0 + lax.erf(values * half_root))
    density = density_scale * jnp.exp(-0.5 * values * values)
    return (values * normal_cdf, normal_cdf + values * density, density * (2.0 - values * values))


def load(arrays):
    count = len(arrays)

    def kernel(*refs):
        sources, targets, sems = refs[:count], refs[count : 2 * count], refs[2 * count]
        copies = [
            pltpu.make_async_copy(source, target, sems.at[i])
            for i, (source, target) in enumerate(zip(sources, targets))
        ]
        for copy in copies:
            copy.start()
        for copy in copies:
            copy.wait()

    return pl.pallas_call(
        kernel,
        out_shape=tuple(pltpu.VMEM(a.shape, a.dtype) for a in arrays),
        in_specs=[ANYWHERE] * count,
        out_specs=(IN_VMEM,) * count,
        scratch_shapes=[pltpu.SemaphoreType.DMA((count,))],
        compiler_params=pltpu.CompilerParams(vmem_limit_bytes=1 << 20),
        name="load",
    )(*[hbm(a) for a in arrays])


def blank(shapes):
    def kernel(*refs):
        refs[-1][...] = jnp.zeros(refs[-1].shape, refs[-1].dtype)

    return pl.pallas_call(
        kernel,
        out_shape=tuple(pltpu.VMEM(shape, kind) for shape, kind in shapes),
        out_specs=(IN_VMEM,) * len(shapes),
        compiler_params=pltpu.CompilerParams(vmem_limit_bytes=1 << 20),
        name="blank",
    )()


class Plan:
    def __init__(self, layers, pieces, lag):
        self.layers, self.pieces, self.lag = layers, pieces, lag
        self.ticks = 2 * layers + lag + pieces - 1

    def stages(self, first, step):
        found = [first - step * m for m in range(self.pieces)]
        return [s for s in found if 0 <= s < self.layers]

    def forward(self, t):
        return self.stages(t, 1)

    def forward_tan(self, t):
        return self.stages(t - self.lag, 1)

    def backward(self, t):
        return self.stages(2 * self.layers - 1 - t, -1)

    def backward_tan(self, t):
        return self.stages(2 * self.layers - 1 - t + self.lag, -1)

    def ready_forward(self, t):
        return 0 <= t - (self.lag - 1) < self.layers

    def ready_backward(self, t):
        return 0 <= 2 * self.layers - 2 + self.lag - t < self.layers

    def waves(self, t):
        found = {}
        for name, stages, way in (
            ("tan_up", self.forward_tan(t), 1),
            ("tan_down", self.backward_tan(t), -1),
            ("up", self.forward(t), 1),
            ("down", self.backward(t), -1),
        ):
            if stages:
                found[name] = [(s, s + way) for s in stages if 0 <= s + way < self.layers]
        return found


def tick_kernel(plan, t, with_probes, loss_scale, rows, width, hidden, *refs):
    refs = list(refs[5:])
    waves = plan.waves(t)
    w_up, w_down, source, goal = refs[:4]
    refs = refs[4:]
    if with_probes:
        u_up, u_down = refs[:2]
        refs = refs[2:]
    got = {name: refs.pop(0) for name in waves}
    sb_d, sb_f, sf_d, sf_f, sf_n = refs[:5]
    put_up, put_down = refs[5:]

    layers, pieces, lag = plan.layers, plan.pieces, plan.lag
    stage = lax.axis_index("pipe")
    at_first, at_last = stage == 0, stage == layers - 1
    chunks = [slice(c, c + CHUNK) for c in range(0, hidden, CHUNK)]
    lanes = (rows, 128)

    def when_due(piece, work):
        @pl.when((piece >= 0) & (piece < pieces))
        def _():
            work(pl.ds(pl.multiple_of(jnp.clip(piece, 0, pieces - 1) * rows, rows), rows))

    def spread(value):
        return jnp.broadcast_to(value, lanes)

    def narrow(slot, at):
        return sf_n[slot, at, :][:, :1]

    def forward(at):
        stream = jnp.where(at_first, source[at, :], got["up"][...]).astype(f32)
        centre = stream - mean(stream)
        inverse = lax.rsqrt(mean(centre * centre) + epsilon)
        normed = centre * inverse
        sf_d[XH, at, :] = normed
        sf_n[INV, at, :] = spread(inverse)
        normed_b = normed.astype(bf16)
        sb_d[X, at, :] = normed_b
        total = stream
        for c in chunks:
            active, slope, curve = gelu_terms(dot(normed_b, w_up[:, c]))
            active_b = active.astype(bf16)
            sb_f[A, at, c] = active_b
            sf_f[SLOPE, at, c] = slope
            sf_f[CURVE, at, c] = curve
            total = total + dot(active_b, w_down[c, :])
        result = total.astype(bf16)

        @pl.when(jnp.logical_not(at_last))
        def _():
            put_up[...] = result

        @pl.when(at_last)
        def _():
            gap = result.astype(f32) - goal[at, :].astype(f32)
            sb_d[G, at, :] = (gap * loss_scale).astype(bf16)

    def ready_forward():
        for c in chunks:
            sf_f[XU, :, c] = dot(sb_d[X], u_up[:, c])
        for c in [slice(c, c + CHUNK) for c in range(0, width, CHUNK)]:
            sf_d[AV, :, c] = dot_last(sb_f[A], u_down[c, :])

    def forward_tan(at):
        tangent = got["tan_up"][...].astype(f32)
        tangent = jnp.where(at_first, jnp.zeros_like(tangent), tangent)
        normed = sf_d[XH, at, :]
        inverse = narrow(INV, at)
        centre = tangent - mean(tangent)
        ratio = mean(normed * centre)
        normed_t = inverse * (centre - normed * ratio)
        sf_d[TXF, at, :] = normed_t
        sf_n[RR, at, :] = spread(-inverse * ratio)
        normed_tb = normed_t.astype(bf16)
        sb_d[TX, at, :] = normed_tb
        total = tangent + sf_d[AV, at, :]
        for c in chunks:
            pre_tan = dot(normed_tb, w_up[:, c]) + sf_f[XU, at, c]
            sf_f[TY, at, c] = pre_tan
            active_tb = (sf_f[SLOPE, at, c] * pre_tan).astype(bf16)
            sb_f[TA, at, c] = active_tb
            total = total + dot(active_tb, w_down[c, :])
        result = total.astype(bf16)

        @pl.when(jnp.logical_not(at_last))
        def _():
            put_up[...] = result

        @pl.when(at_last)
        def _():
            sb_d[TG, at, :] = (result.astype(f32) * loss_scale).astype(bf16)

    def backward(at):
        cotan = jnp.where(at_last, sb_d[G, at, :], got["down"][...])
        sb_d[G, at, :] = cotan
        grad = jnp.zeros((rows, width), f32)
        for c in chunks:
            grad_act = dot_last(cotan, w_down[c, :])
            sf_f[CC, at, c] = grad_act * sf_f[CURVE, at, c]
            grad_pre = (grad_act * sf_f[SLOPE, at, c]).astype(bf16)
            sb_f[PR, at, c] = grad_pre
            grad = grad + dot_last(grad_pre, w_up[:, c])
        sf_d[QN, at, :] = grad
        normed = sf_d[XH, at, :]
        along = mean(grad * normed)
        sf_n[M1, at, :] = spread(along)
        back = narrow(INV, at) * (grad - mean(grad) - normed * along)
        sf_d[BN, at, :] = back
        result = (cotan.astype(f32) + back).astype(bf16)

        @pl.when(jnp.logical_not(at_first))
        def _():
            put_down[...] = result

    def ready_backward():
        for c in chunks:
            sf_f[GV, :, c] = dot(sb_d[G], u_down[:, c])
        for c in [slice(c, c + CHUNK) for c in range(0, width, CHUNK)]:
            sf_d[PU, :, c] = dot_last(sb_f[PR], u_up[c, :])

    def backward_tan(at):
        cotan_t = jnp.where(at_last, sb_d[TG, at, :], got["tan_down"][...])
        sb_d[TG, at, :] = cotan_t
        grad_t = sf_d[PU, at, :]
        for c in chunks:
            grad_act_t = dot_last(cotan_t, w_down[c, :]) + sf_f[GV, at, c]
            grad_pre_t = grad_act_t * sf_f[SLOPE, at, c] + sf_f[CC, at, c] * sf_f[TY, at, c]
            grad_pre_tb = grad_pre_t.astype(bf16)
            sb_f[TP, at, c] = grad_pre_tb
            grad_t = grad_t + dot_last(grad_pre_tb, w_up[:, c])
        normed, normed_t, inverse = sf_d[XH, at, :], sf_d[TXF, at, :], narrow(INV, at)
        along_t = mean(grad_t * normed + sf_d[QN, at, :] * normed_t)
        inner = grad_t - mean(grad_t) - normed_t * narrow(M1, at) - normed * along_t
        back_t = narrow(RR, at) * sf_d[BN, at, :] + inverse * inner
        result = (cotan_t.astype(f32) + back_t).astype(bf16)

        @pl.when(jnp.logical_not(at_first))
        def _():
            put_down[...] = result

    if plan.backward_tan(t):
        when_due(t - lag - (2 * layers - 1 - stage), backward_tan)
    if plan.forward_tan(t):
        when_due(t - lag - stage, forward_tan)
    if plan.backward(t):
        when_due(t - (2 * layers - 1 - stage), backward)
    if plan.forward(t):
        when_due(t - stage, forward)
    if plan.ready_forward(t):
        pl.when(stage == t - (lag - 1))(ready_forward)
    if plan.ready_backward(t):
        pl.when(stage == 2 * layers - 2 + lag - t)(ready_backward)


BATCHES = ((4,), (3, 5), (2, 6), (1, 7, 0))


def curvature_kernel(sb_d, sb_f, *refs):
    mine, theirs = refs[: len(BATCHES)], refs[len(BATCHES) : 2 * len(BATCHES)]
    hold = refs[-1]
    hidden = sb_f.shape[2]
    here = lax.axis_index("dp")
    chip, core = here // 2, lax.rem(here, 2)
    chips = lax.axis_size("dp") // 2
    step = hold.shape[0]
    part = step // 2
    for kept, given, batch in zip(mine, theirs, BATCHES):
        for i, far in enumerate(batch):
            at = pl.ds(pl.multiple_of(lax.rem(chip + far, chips) * step, step), step)
            left = jnp.concatenate((sb_d[X, :, at], sb_d[TX, :, at]), axis=0)
            right = jnp.concatenate((sb_f[TP], sb_f[PR]), axis=0)
            hold[:, :hidden] = dot_first(left, right)
            left = jnp.concatenate((sb_d[TG, :, at], sb_d[G, :, at]), axis=0)
            right = jnp.concatenate((sb_f[A], sb_f[TA]), axis=0)
            hold[:, hidden:] = dot_first(left, right)
            kept[i] = hold[pl.ds(pl.multiple_of(core * part, part), part), :].astype(bf16)
            given[i] = hold[pl.ds(pl.multiple_of((1 - core) * part, part), part), :].astype(bf16)


def curvature(sb_d, sb_f, groups):
    width, hidden = sb_d.shape[2], sb_f.shape[2]
    part = width // groups
    parts = tuple(pltpu.VMEM((len(batch), part, 2 * hidden), bf16) for batch in BATCHES)
    outs = pl.pallas_call(
        curvature_kernel,
        out_shape=parts + parts,
        in_specs=[IN_VMEM, IN_VMEM],
        out_specs=(IN_VMEM,) * (2 * len(BATCHES)),
        scratch_shapes=[pltpu.VMEM((2 * part, 2 * hidden), f32)],
        compiler_params=pltpu.CompilerParams(vmem_limit_bytes=12 << 20),
        name="curvature",
    )(vmem(sb_d), vmem(sb_f))
    return outs[: len(BATCHES)], outs[len(BATCHES) :]


def routes(groups):
    return (
        [(i, (i + 2) % groups) for i in range(groups)],
        [(i, (i - 2) % groups) for i in range(groups)],
        [(i, i ^ 1) for i in range(groups)],
    )


def assemble(blocks, halves, groups, part, hidden):
    pieces = [(array, i, (i,), far, other) for array, far, other in blocks for i in range(2)]
    pieces += [(array, i, (), far, other) for array, i, far, other in halves]
    arrays = [b[0] for b in blocks] + [h[0] for h in halves]
    places = [p for p in range(len(blocks)) for _ in range(2)] + [len(blocks) + p for p in range(len(halves))]

    def kernel(*refs):
        sources, targets, sems = refs[: len(arrays)], refs[len(arrays) : -1], refs[-1]
        here = lax.axis_index("dp")
        chip, core = here // 2, lax.rem(here, 2)
        chips = groups // 2
        copies = []
        for n, ((_, probe, index, far, other), place) in enumerate(zip(pieces, places)):
            block = lax.rem(chip + far + chips, chips) * 2 + (1 - core if other else core)
            row = pl.ds(pl.multiple_of(block * part, part), part)
            source = sources[place].at[index] if index else sources[place]
            copies.append(pltpu.make_async_copy(source, targets[probe].at[row, :], sems.at[n]))
        for copy in copies:
            copy.start()
        for copy in copies:
            copy.wait()

    return pl.pallas_call(
        kernel,
        out_shape=tuple(pltpu.VMEM((groups * part, hidden), bf16) for _ in range(2)),
        in_specs=[ANYWHERE] * len(arrays),
        out_specs=(IN_VMEM,) * 2,
        scratch_shapes=[pltpu.SemaphoreType.DMA((len(pieces),))],
        compiler_params=pltpu.CompilerParams(vmem_limit_bytes=1 << 20),
        name="assemble",
    )(*arrays)


def scatter(mine, theirs, groups, hidden):
    ahead, behind, across = routes(groups)

    def wide(kept, given):
        return kept.astype(f32) + lax.ppermute(given, "dp", across).astype(f32)

    far = wide(mine[0], theirs[0])[0].astype(bf16)
    from_behind = lax.ppermute(far[:, :hidden], "dp", ahead)
    from_ahead = lax.ppermute(far[:, hidden:], "dp", behind)
    blank_half = ((0, 0), (0, hidden)), ((0, 0), (hidden, 0))
    pair = wide(mine[1], theirs[1])
    up = (pair[0] + jnp.pad(from_behind.astype(f32), blank_half[0])).astype(bf16)
    down = (pair[1] + jnp.pad(from_ahead.astype(f32), blank_half[1])).astype(bf16)
    for kept, given in zip(mine[2:], theirs[2:]):
        from_behind = lax.ppermute(up, "dp", ahead)
        from_ahead = lax.ppermute(down, "dp", behind)
        pair = wide(kept, given)
        up = (pair[0] + from_behind.astype(f32)).astype(bf16)
        down = (pair[1] + from_ahead.astype(f32)).astype(bf16)
    from_behind = lax.ppermute(up, "dp", ahead)
    from_ahead = lax.ppermute(down, "dp", behind)
    return pair[2] + from_behind.astype(f32) + from_ahead.astype(f32)


def on_device(embedded, targets, w_up, w_down, probe_up, probe_down):
    layers = lax.axis_size("pipe")
    groups = lax.axis_size("dp")
    tokens, width = embedded.shape
    hidden = w_up.shape[2]
    part = probe_up.shape[1]
    rows = tokens // PIECES
    loss_scale = 1.0 / (tokens * groups)
    plan = Plan(layers, PIECES, LAG)
    ahead, behind, across = routes(groups)

    def swap(array):
        return lax.ppermute(array, "dp", across)

    def ring(both):
        return [lax.ppermute(both[0], "dp", ahead), lax.ppermute(both[1], "dp", behind)]

    own = jnp.stack((probe_up[0], probe_down[0]))
    moving = ring([own, own])
    blocks = [(own, 0, False), (swap(own), 0, True)]
    halves = []

    held = load((w_up[0], w_down[0], embedded, targets))
    *state, nothing = blank(
        (
            ((4, tokens, width), bf16),
            ((4, tokens, hidden), bf16),
            ((6, tokens, width), f32),
            ((6, tokens, hidden), f32),
            ((3, tokens, 128), f32),
            ((rows, width), bf16),
        )
    )
    probes = None
    got = {"up": nothing}
    packet = pltpu.VMEM((rows, width), bf16)
    ring_ticks = {0: 1, 2: 2, 3: 3, 4: 4}
    for t in range(plan.ticks):
        if t == LAG - 1:
            probes = assemble(blocks, halves, groups, part, hidden)
        waves = plan.waves(t)
        with_probes = plan.ready_forward(t) or plan.ready_backward(t)
        operands = list(state) + list(held) + (list(probes) if with_probes else [])
        operands += [got.get(name, nothing) for name in waves]
        outs = pl.pallas_call(
            functools.partial(tick_kernel, plan, t, with_probes, loss_scale, rows, width, hidden),
            out_shape=tuple(pltpu.VMEM(s.shape, s.dtype) for s in state) + (packet,) * 2,
            in_specs=[IN_VMEM] * len(operands),
            out_specs=(IN_VMEM,) * 7,
            input_output_aliases={i: i for i in range(5)},
            compiler_params=pltpu.CompilerParams(vmem_limit_bytes=8 << 20),
            cost_estimate=pl.CostEstimate(flops=1 << 30, bytes_accessed=1 << 23, transcendentals=0),
            name="tick",
        )(*[vmem(o) for o in operands])
        state, sent = outs[:5], {"up": outs[5], "down": outs[6]}
        got = {
            name: lax.ppermute(sent[name.removeprefix("tan_")], "pipe", edges)
            for name, edges in waves.items()
            if edges
        }
        if t in ring_ticks:
            step = ring_ticks[t]
            got["up"], moving[0], moving[1] = lax.optimization_barrier((got["up"], *moving))
            if step < 4:
                arrived = moving
                moving = ring(arrived if step < 3 else [arrived[0][0], arrived[1][1]])
                for array, away in zip(arrived, (-step, step)):
                    blocks += [(array, away, False), (swap(array), away, True)]
            else:
                for i, array in enumerate(moving):
                    halves += [(array, i, step, False), (swap(array), i, step, True)]

    mine, theirs = curvature(state[0], state[1], groups)
    summed = scatter(mine, theirs, groups, hidden)
    curv_up = probe_up[0].astype(f32) * summed[:, :hidden]
    curv_down = probe_down[0].astype(f32) * summed[:, hidden:]
    return (curv_up[None], curv_down[None])


def solution(mesh):
    in_specs = (
        P("dp", None),
        P("dp", None),
        P("pipe", None, None),
        P("pipe", None, None),
        P("pipe", "dp", None),
        P("pipe", "dp", None),
    )
    out_specs = (P("pipe", "dp", None), P("pipe", "dp", None))
    return jax.shard_map(
        on_device, mesh=mesh, in_specs=in_specs, out_specs=out_specs, check_vma=False
    )
```

```python
import functools

import jax
import jax.numpy as jnp
from jax import lax
from jax.experimental import pallas as pl
from jax.experimental.pallas import tpu as pltpu
from jax.sharding import PartitionSpec as P

PIECES = 4
LAG = 7
CHUNK = 512

epsilon = 1e-05
half_root = 0.7071067811865476
density_scale = 0.3989422804014327

f32 = jnp.float32
bf16 = jnp.bfloat16

X, TX, G, TG = range(4)
A, TA, PR, TP = range(4)
XH, TXF, QN, BN, PU, AV = range(6)
SLOPE, CURVE, TY, XU, CC, GV = range(6)
INV, RR, M1 = range(3)

IN_VMEM = pl.BlockSpec(memory_space=pltpu.VMEM)
ANYWHERE = pl.BlockSpec(memory_space=pl.ANY)


def vmem(array):
    return pltpu.with_memory_space_constraint(array, pltpu.VMEM)


def hbm(array):
    return pltpu.with_memory_space_constraint(array, pltpu.HBM)


def dot(left, right):
    return jnp.dot(left, right, preferred_element_type=f32)


def dot_last(left, right):
    return lax.dot_general(left, right, (((1,), (1,)), ((), ())), preferred_element_type=f32)


def dot_first(left, right):
    return lax.dot_general(left, right, (((0,), (0,)), ((), ())), preferred_element_type=f32)


def mean(values):
    return jnp.mean(values, axis=-1, keepdims=True)


def gelu_terms(values):
    normal_cdf = 0.5 * (1.0 + lax.erf(values * half_root))
    density = density_scale * jnp.exp(-0.5 * values * values)
    return (values * normal_cdf, normal_cdf + values * density, density * (2.0 - values * values))


def load(arrays):
    count = len(arrays)

    def kernel(*refs):
        sources, targets, sems = refs[:count], refs[count : 2 * count], refs[2 * count]
        copies = [
            pltpu.make_async_copy(source, target, sems.at[i])
            for i, (source, target) in enumerate(zip(sources, targets))
        ]
        for copy in copies:
            copy.start()
        for copy in copies:
            copy.wait()

    return pl.pallas_call(
        kernel,
        out_shape=tuple(pltpu.VMEM(a.shape, a.dtype) for a in arrays),
        in_specs=[ANYWHERE] * count,
        out_specs=(IN_VMEM,) * count,
        scratch_shapes=[pltpu.SemaphoreType.DMA((count,))],
        compiler_params=pltpu.CompilerParams(vmem_limit_bytes=1 << 20),
        name="load",
    )(*[hbm(a) for a in arrays])


def blank(shapes):
    def kernel(*refs):
        refs[-1][...] = jnp.zeros(refs[-1].shape, refs[-1].dtype)

    return pl.pallas_call(
        kernel,
        out_shape=tuple(pltpu.VMEM(shape, kind) for shape, kind in shapes),
        out_specs=(IN_VMEM,) * len(shapes),
        compiler_params=pltpu.CompilerParams(vmem_limit_bytes=1 << 20),
        name="blank",
    )()


class Plan:
    def __init__(self, layers, pieces, lag):
        self.layers, self.pieces, self.lag = layers, pieces, lag
        self.ticks = 2 * layers + lag + pieces - 1

    def stages(self, first, step):
        found = [first - step * m for m in range(self.pieces)]
        return [s for s in found if 0 <= s < self.layers]

    def forward(self, t):
        return self.stages(t, 1)

    def forward_tan(self, t):
        return self.stages(t - self.lag, 1)

    def backward(self, t):
        return self.stages(2 * self.layers - 1 - t, -1)

    def backward_tan(self, t):
        return self.stages(2 * self.layers - 1 - t + self.lag, -1)

    def ready_forward(self, t):
        return 0 <= t - (self.lag - 1) < self.layers

    def ready_backward(self, t):
        return 0 <= 2 * self.layers - 2 + self.lag - t < self.layers

    def waves(self, t):
        found = {}
        count = min(self.pieces, self.layers - 1)
        for name, stages, way in (
            ("tan_up", self.forward_tan(t), 1),
            ("tan_down", self.backward_tan(t), -1),
            ("up", self.forward(t), 1),
            ("down", self.backward(t), -1),
        ):
            if stages:
                useful = [(s, s + way) for s in stages if 0 <= s + way < self.layers]
                lowest = min([min(e) for e in useful], default=0)
                lowest = min(lowest, self.layers - 1 - count)
                pairs = [(s, s + 1) for s in range(lowest, lowest + count)] if useful else []
                found[name] = pairs if way > 0 else [(r, s) for s, r in pairs]
                assert set(useful) <= set(found[name])
        return found


def tick_kernel(plan, t, with_probes, loss_scale, rows, width, hidden, *refs):
    refs = list(refs[5:])
    waves = plan.waves(t)
    w_up, w_down, source, goal = refs[:4]
    refs = refs[4:]
    if with_probes:
        u_up, u_down = refs[:2]
        refs = refs[2:]
    got = {name: refs.pop(0) for name in waves}
    sb_d, sb_f, sf_d, sf_f, sf_n = refs[:5]
    put_up, put_down = refs[5:]

    layers, pieces, lag = plan.layers, plan.pieces, plan.lag
    stage = lax.axis_index("pipe")
    at_first, at_last = stage == 0, stage == layers - 1
    chunks = [slice(c, c + CHUNK) for c in range(0, hidden, CHUNK)]
    lanes = (rows, 128)

    def when_due(piece, work):
        @pl.when((piece >= 0) & (piece < pieces))
        def _():
            work(pl.ds(pl.multiple_of(jnp.clip(piece, 0, pieces - 1) * rows, rows), rows))

    def spread(value):
        return jnp.broadcast_to(value, lanes)

    def narrow(slot, at):
        return sf_n[slot, at, :][:, :1]

    def forward(at):
        stream = jnp.where(at_first, source[at, :], got["up"][...]).astype(f32)
        centre = stream - mean(stream)
        inverse = lax.rsqrt(mean(centre * centre) + epsilon)
        normed = centre * inverse
        sf_d[XH, at, :] = normed
        sf_n[INV, at, :] = spread(inverse)
        normed_b = normed.astype(bf16)
        sb_d[X, at, :] = normed_b
        total = stream
        for c in chunks:
            active, slope, curve = gelu_terms(dot(normed_b, w_up[:, c]))
            active_b = active.astype(bf16)
            sb_f[A, at, c] = active_b
            sf_f[SLOPE, at, c] = slope
            sf_f[CURVE, at, c] = curve
            total = total + dot(active_b, w_down[c, :])
        result = total.astype(bf16)

        @pl.when(jnp.logical_not(at_last))
        def _():
            put_up[...] = result

        @pl.when(at_last)
        def _():
            gap = result.astype(f32) - goal[at, :].astype(f32)
            sb_d[G, at, :] = (gap * loss_scale).astype(bf16)

    def ready_forward():
        for c in chunks:
            sf_f[XU, :, c] = dot(sb_d[X], u_up[:, c])
        for c in [slice(c, c + CHUNK) for c in range(0, width, CHUNK)]:
            sf_d[AV, :, c] = dot_last(sb_f[A], u_down[c, :])

    def forward_tan(at):
        tangent = got["tan_up"][...].astype(f32)
        tangent = jnp.where(at_first, jnp.zeros_like(tangent), tangent)
        normed = sf_d[XH, at, :]
        inverse = narrow(INV, at)
        centre = tangent - mean(tangent)
        ratio = mean(normed * centre)
        normed_t = inverse * (centre - normed * ratio)
        sf_d[TXF, at, :] = normed_t
        sf_n[RR, at, :] = spread(-inverse * ratio)
        normed_tb = normed_t.astype(bf16)
        sb_d[TX, at, :] = normed_tb
        total = tangent + sf_d[AV, at, :]
        for c in chunks:
            pre_tan = dot(normed_tb, w_up[:, c]) + sf_f[XU, at, c]
            sf_f[TY, at, c] = pre_tan
            active_tb = (sf_f[SLOPE, at, c] * pre_tan).astype(bf16)
            sb_f[TA, at, c] = active_tb
            total = total + dot(active_tb, w_down[c, :])
        result = total.astype(bf16)

        @pl.when(jnp.logical_not(at_last))
        def _():
            put_up[...] = result

        @pl.when(at_last)
        def _():
            sb_d[TG, at, :] = (result.astype(f32) * loss_scale).astype(bf16)

    def backward(at):
        cotan = jnp.where(at_last, sb_d[G, at, :], got["down"][...])
        sb_d[G, at, :] = cotan
        grad = jnp.zeros((rows, width), f32)
        for c in chunks:
            grad_act = dot_last(cotan, w_down[c, :])
            sf_f[CC, at, c] = grad_act * sf_f[CURVE, at, c]
            grad_pre = (grad_act * sf_f[SLOPE, at, c]).astype(bf16)
            sb_f[PR, at, c] = grad_pre
            grad = grad + dot_last(grad_pre, w_up[:, c])
        sf_d[QN, at, :] = grad
        normed = sf_d[XH, at, :]
        along = mean(grad * normed)
        sf_n[M1, at, :] = spread(along)
        back = narrow(INV, at) * (grad - mean(grad) - normed * along)
        sf_d[BN, at, :] = back
        result = (cotan.astype(f32) + back).astype(bf16)

        @pl.when(jnp.logical_not(at_first))
        def _():
            put_down[...] = result

    def ready_backward():
        for c in chunks:
            sf_f[GV, :, c] = dot(sb_d[G], u_down[:, c])
        for c in [slice(c, c + CHUNK) for c in range(0, width, CHUNK)]:
            sf_d[PU, :, c] = dot_last(sb_f[PR], u_up[c, :])

    def backward_tan(at):
        cotan_t = jnp.where(at_last, sb_d[TG, at, :], got["tan_down"][...])
        sb_d[TG, at, :] = cotan_t
        grad_t = sf_d[PU, at, :]
        for c in chunks:
            grad_act_t = dot_last(cotan_t, w_down[c, :]) + sf_f[GV, at, c]
            grad_pre_t = grad_act_t * sf_f[SLOPE, at, c] + sf_f[CC, at, c] * sf_f[TY, at, c]
            grad_pre_tb = grad_pre_t.astype(bf16)
            sb_f[TP, at, c] = grad_pre_tb
            grad_t = grad_t + dot_last(grad_pre_tb, w_up[:, c])
        normed, normed_t, inverse = sf_d[XH, at, :], sf_d[TXF, at, :], narrow(INV, at)
        along_t = mean(grad_t * normed + sf_d[QN, at, :] * normed_t)
        inner = grad_t - mean(grad_t) - normed_t * narrow(M1, at) - normed * along_t
        back_t = narrow(RR, at) * sf_d[BN, at, :] + inverse * inner
        result = (cotan_t.astype(f32) + back_t).astype(bf16)

        @pl.when(jnp.logical_not(at_first))
        def _():
            put_down[...] = result

    if plan.backward_tan(t):
        when_due(t - lag - (2 * layers - 1 - stage), backward_tan)
    if plan.forward_tan(t):
        when_due(t - lag - stage, forward_tan)
    if plan.backward(t):
        when_due(t - (2 * layers - 1 - stage), backward)
    if plan.forward(t):
        when_due(t - stage, forward)
    if plan.ready_forward(t):
        pl.when(stage == t - (lag - 1))(ready_forward)
    if plan.ready_backward(t):
        pl.when(stage == 2 * layers - 2 + lag - t)(ready_backward)


BATCHES = ((4,), (3, 5), (2, 6), (1, 7, 0))


def curvature_kernel(sb_d, sb_f, *refs):
    mine, theirs = refs[: len(BATCHES)], refs[len(BATCHES) : 2 * len(BATCHES)]
    hold = refs[-1]
    hidden = sb_f.shape[2]
    here = lax.axis_index("dp")
    chip, core = here // 2, lax.rem(here, 2)
    chips = lax.axis_size("dp") // 2
    step = hold.shape[0]
    part = step // 2
    for kept, given, batch in zip(mine, theirs, BATCHES):
        for i, far in enumerate(batch):
            at = pl.ds(pl.multiple_of(lax.rem(chip + far, chips) * step, step), step)
            left = jnp.concatenate((sb_d[X, :, at], sb_d[TX, :, at]), axis=0)
            right = jnp.concatenate((sb_f[TP], sb_f[PR]), axis=0)
            hold[:, :hidden] = dot_first(left, right)
            left = jnp.concatenate((sb_d[TG, :, at], sb_d[G, :, at]), axis=0)
            right = jnp.concatenate((sb_f[A], sb_f[TA]), axis=0)
            hold[:, hidden:] = dot_first(left, right)
            kept[i] = hold[pl.ds(pl.multiple_of(core * part, part), part), :].astype(bf16)
            given[i] = hold[pl.ds(pl.multiple_of((1 - core) * part, part), part), :].astype(bf16)


def curvature(sb_d, sb_f, groups):
    width, hidden = sb_d.shape[2], sb_f.shape[2]
    part = width // groups
    parts = tuple(pltpu.VMEM((len(batch), part, 2 * hidden), bf16) for batch in BATCHES)
    outs = pl.pallas_call(
        curvature_kernel,
        out_shape=parts + parts,
        in_specs=[IN_VMEM, IN_VMEM],
        out_specs=(IN_VMEM,) * (2 * len(BATCHES)),
        scratch_shapes=[pltpu.VMEM((2 * part, 2 * hidden), f32)],
        compiler_params=pltpu.CompilerParams(vmem_limit_bytes=12 << 20),
        name="curvature",
    )(vmem(sb_d), vmem(sb_f))
    return outs[: len(BATCHES)], outs[len(BATCHES) :]


def routes(groups):
    return (
        [(i, (i + 2) % groups) for i in range(groups)],
        [(i, (i - 2) % groups) for i in range(groups)],
        [(i, i ^ 1) for i in range(groups)],
    )


def assemble(blocks, halves, groups, part, hidden):
    pieces = [(array, i, (i,), far, other) for array, far, other in blocks for i in range(2)]
    pieces += [(array, i, (), far, other) for array, i, far, other in halves]
    arrays = [b[0] for b in blocks] + [h[0] for h in halves]
    places = [p for p in range(len(blocks)) for _ in range(2)] + [len(blocks) + p for p in range(len(halves))]

    def kernel(*refs):
        sources, targets, sems = refs[: len(arrays)], refs[len(arrays) : -1], refs[-1]
        here = lax.axis_index("dp")
        chip, core = here // 2, lax.rem(here, 2)
        chips = groups // 2
        copies = []
        for n, ((_, probe, index, far, other), place) in enumerate(zip(pieces, places)):
            block = lax.rem(chip + far + chips, chips) * 2 + (1 - core if other else core)
            row = pl.ds(pl.multiple_of(block * part, part), part)
            source = sources[place].at[index] if index else sources[place]
            copies.append(pltpu.make_async_copy(source, targets[probe].at[row, :], sems.at[n]))
        for copy in copies:
            copy.start()
        for copy in copies:
            copy.wait()

    return pl.pallas_call(
        kernel,
        out_shape=tuple(pltpu.VMEM((groups * part, hidden), bf16) for _ in range(2)),
        in_specs=[ANYWHERE] * len(arrays),
        out_specs=(IN_VMEM,) * 2,
        scratch_shapes=[pltpu.SemaphoreType.DMA((len(pieces),))],
        compiler_params=pltpu.CompilerParams(vmem_limit_bytes=1 << 20),
        name="assemble",
    )(*arrays)


def scatter(mine, theirs, groups, hidden):
    ahead, behind, across = routes(groups)

    def wide(kept, given):
        return kept.astype(f32) + lax.ppermute(given, "dp", across).astype(f32)

    far = wide(mine[0], theirs[0])[0].astype(bf16)
    from_behind = lax.ppermute(far[:, :hidden], "dp", ahead)
    from_ahead = lax.ppermute(far[:, hidden:], "dp", behind)
    blank_half = ((0, 0), (0, hidden)), ((0, 0), (hidden, 0))
    pair = wide(mine[1], theirs[1])
    up = (pair[0] + jnp.pad(from_behind.astype(f32), blank_half[0])).astype(bf16)
    down = (pair[1] + jnp.pad(from_ahead.astype(f32), blank_half[1])).astype(bf16)
    for kept, given in zip(mine[2:], theirs[2:]):
        from_behind = lax.ppermute(up, "dp", ahead)
        from_ahead = lax.ppermute(down, "dp", behind)
        pair = wide(kept, given)
        up = (pair[0] + from_behind.astype(f32)).astype(bf16)
        down = (pair[1] + from_ahead.astype(f32)).astype(bf16)
    from_behind = lax.ppermute(up, "dp", ahead)
    from_ahead = lax.ppermute(down, "dp", behind)
    return pair[2] + from_behind.astype(f32) + from_ahead.astype(f32)


def on_device(embedded, targets, w_up, w_down, probe_up, probe_down):
    layers = lax.axis_size("pipe")
    groups = lax.axis_size("dp")
    tokens, width = embedded.shape
    hidden = w_up.shape[2]
    part = probe_up.shape[1]
    rows = tokens // PIECES
    loss_scale = 1.0 / (tokens * groups)
    plan = Plan(layers, PIECES, LAG)
    ahead, behind, across = routes(groups)

    def swap(array):
        return lax.ppermute(array, "dp", across)

    def ring(both):
        return [lax.ppermute(both[0], "dp", ahead), lax.ppermute(both[1], "dp", behind)]

    own = jnp.stack((probe_up[0], probe_down[0]))
    moving = ring([own, own])
    blocks = [(own, 0, False), (swap(own), 0, True)]
    halves = []

    held = load((w_up[0], w_down[0], embedded, targets))
    *state, nothing = blank(
        (
            ((4, tokens, width), bf16),
            ((4, tokens, hidden), bf16),
            ((6, tokens, width), f32),
            ((6, tokens, hidden), f32),
            ((3, tokens, 128), f32),
            ((rows, width), bf16),
        )
    )
    probes = None
    got = {"up": nothing}
    packet = pltpu.VMEM((rows, width), bf16)
    ring_ticks = {0: 1, 1: 2, 2: 3, 3: 4}
    for t in range(plan.ticks):
        if t == LAG - 1:
            probes = assemble(blocks, halves, groups, part, hidden)
        waves = plan.waves(t)
        with_probes = plan.ready_forward(t) or plan.ready_backward(t)
        operands = list(state) + list(held) + (list(probes) if with_probes else [])
        operands += [got.get(name, nothing) for name in waves]
        outs = pl.pallas_call(
            functools.partial(tick_kernel, plan, t, with_probes, loss_scale, rows, width, hidden),
            out_shape=tuple(pltpu.VMEM(s.shape, s.dtype) for s in state) + (packet,) * 2,
            in_specs=[IN_VMEM] * len(operands),
            out_specs=(IN_VMEM,) * 7,
            input_output_aliases={i: i for i in range(5)},
            compiler_params=pltpu.CompilerParams(vmem_limit_bytes=8 << 20),
            cost_estimate=pl.CostEstimate(flops=1 << 30, bytes_accessed=1 << 23, transcendentals=0),
            name="tick",
        )(*[vmem(o) for o in operands])
        state, sent = outs[:5], {"up": outs[5], "down": outs[6]}
        got = {
            name: lax.ppermute(sent[name.removeprefix("tan_")], "pipe", edges)
            for name, edges in waves.items()
            if edges
        }
        if t in ring_ticks:
            step = ring_ticks[t]
            got["up"], moving[0], moving[1] = lax.optimization_barrier((got["up"], *moving))
            if step < 4:
                arrived = moving
                moving = ring(arrived if step < 3 else [arrived[0][0], arrived[1][1]])
                for array, away in zip(arrived, (-step, step)):
                    blocks += [(array, away, False), (swap(array), away, True)]
            else:
                for i, array in enumerate(moving):
                    halves += [(array, i, step, False), (swap(array), i, step, True)]

    mine, theirs = curvature(state[0], state[1], groups)
    summed = scatter(mine, theirs, groups, hidden)
    curv_up = probe_up[0].astype(f32) * summed[:, :hidden]
    curv_down = probe_down[0].astype(f32) * summed[:, hidden:]
    return (curv_up[None], curv_down[None])


def solution(mesh):
    in_specs = (
        P("dp", None),
        P("dp", None),
        P("pipe", None, None),
        P("pipe", None, None),
        P("pipe", "dp", None),
        P("pipe", "dp", None),
    )
    out_specs = (P("pipe", "dp", None), P("pipe", "dp", None))
    return jax.shard_map(
        on_device, mesh=mesh, in_specs=in_specs, out_specs=out_specs, check_vma=False
    )
```

```python
import functools

import jax
import jax.numpy as jnp
from jax import lax
from jax.experimental import pallas as pl
from jax.experimental.pallas import tpu as pltpu
from jax.sharding import PartitionSpec as P

PIECES = 4
LAG = 7
CHUNK = 512

epsilon = 1e-05
half_root = 0.7071067811865476
density_scale = 0.3989422804014327

f32 = jnp.float32
bf16 = jnp.bfloat16

X, TX, G, TG = range(4)
A, TA, PR, TP = range(4)
XH, TXF, QN, BN, PU, AV = range(6)
SLOPE, CURVE, TY, XU, CC, GV = range(6)
INV, RR, M1 = range(3)

IN_VMEM = pl.BlockSpec(memory_space=pltpu.VMEM)
ANYWHERE = pl.BlockSpec(memory_space=pl.ANY)


def vmem(array):
    return pltpu.with_memory_space_constraint(array, pltpu.VMEM)


def hbm(array):
    return pltpu.with_memory_space_constraint(array, pltpu.HBM)


def dot(left, right):
    return jnp.dot(left, right, preferred_element_type=f32)


def dot_last(left, right):
    return lax.dot_general(left, right, (((1,), (1,)), ((), ())), preferred_element_type=f32)


def dot_first(left, right):
    return lax.dot_general(left, right, (((0,), (0,)), ((), ())), preferred_element_type=f32)


def mean(values):
    return jnp.mean(values, axis=-1, keepdims=True)


def gelu_terms(values):
    normal_cdf = 0.5 * (1.0 + lax.erf(values * half_root))
    density = density_scale * jnp.exp(-0.5 * values * values)
    return (values * normal_cdf, normal_cdf + values * density, density * (2.0 - values * values))


def load(arrays):
    count = len(arrays)

    def kernel(*refs):
        sources, targets, sems = refs[:count], refs[count : 2 * count], refs[2 * count]
        copies = [
            pltpu.make_async_copy(source, target, sems.at[i])
            for i, (source, target) in enumerate(zip(sources, targets))
        ]
        for copy in copies:
            copy.start()
        for copy in copies:
            copy.wait()

    return pl.pallas_call(
        kernel,
        out_shape=tuple(pltpu.VMEM(a.shape, a.dtype) for a in arrays),
        in_specs=[ANYWHERE] * count,
        out_specs=(IN_VMEM,) * count,
        scratch_shapes=[pltpu.SemaphoreType.DMA((count,))],
        compiler_params=pltpu.CompilerParams(vmem_limit_bytes=1 << 20),
        name="load",
    )(*[hbm(a) for a in arrays])


def blank(shapes):
    def kernel(*refs):
        refs[-1][...] = jnp.zeros(refs[-1].shape, refs[-1].dtype)

    return pl.pallas_call(
        kernel,
        out_shape=tuple(pltpu.VMEM(shape, kind) for shape, kind in shapes),
        out_specs=(IN_VMEM,) * len(shapes),
        compiler_params=pltpu.CompilerParams(vmem_limit_bytes=1 << 20),
        name="blank",
    )()


class Plan:
    def __init__(self, layers, pieces, lag):
        self.layers, self.pieces, self.lag = layers, pieces, lag
        self.ticks = 2 * layers + lag + pieces - 1

    def stages(self, first, step):
        found = [first - step * m for m in range(self.pieces)]
        return [s for s in found if 0 <= s < self.layers]

    def forward(self, t):
        return self.stages(t, 1)

    def forward_tan(self, t):
        return self.stages(t - self.lag, 1)

    def backward(self, t):
        return self.stages(2 * self.layers - 1 - t, -1)

    def backward_tan(self, t):
        return self.stages(2 * self.layers - 1 - t + self.lag, -1)

    def ready_forward(self, t):
        return 0 <= t - (self.lag - 1) < self.layers

    def ready_backward(self, t):
        return 0 <= 2 * self.layers - 2 + self.lag - t < self.layers

    def waves(self, t):
        found = {}
        for name, stages, way in (
            ("tan_up", self.forward_tan(t), 1),
            ("tan_down", self.backward_tan(t), -1),
            ("up", self.forward(t), 1),
            ("down", self.backward(t), -1),
        ):
            if stages:
                useful = [(s, s + way) for s in stages if 0 <= s + way < self.layers]
                if way < 0 and useful and useful[0][1] == 0:
                    useful = [(s, s - 1) for s in range(1, min(self.pieces + 1, self.layers))]
                found[name] = useful
        return found


def sends(waves, way):
    return bool(waves.get(way)) or bool(waves.get("tan_" + way))


def tick_kernel(plan, t, with_probes, loss_scale, rows, width, hidden, *refs):
    refs = list(refs[5:])
    waves = plan.waves(t)
    w_up, w_down, source, goal = refs[:4]
    refs = refs[4:]
    if with_probes:
        u_up, u_down = refs[:2]
        refs = refs[2:]
    got = {name: refs.pop(0) for name in waves}
    sb_d, sb_f, sf_d, sf_f, sf_n = refs[:5]
    refs = refs[5:]
    put_up = refs.pop(0) if sends(waves, "up") else None
    put_down = refs.pop(0) if sends(waves, "down") else None

    layers, pieces, lag = plan.layers, plan.pieces, plan.lag
    stage = lax.axis_index("pipe")
    at_first, at_last = stage == 0, stage == layers - 1
    chunks = [slice(c, c + CHUNK) for c in range(0, hidden, CHUNK)]
    lanes = (rows, 128)

    def when_due(piece, work):
        @pl.when((piece >= 0) & (piece < pieces))
        def _():
            work(pl.ds(pl.multiple_of(jnp.clip(piece, 0, pieces - 1) * rows, rows), rows))

    def spread(value):
        return jnp.broadcast_to(value, lanes)

    def narrow(slot, at):
        return sf_n[slot, at, :][:, :1]

    def forward(at):
        stream = jnp.where(at_first, source[at, :], got["up"][...]).astype(f32)
        centre = stream - mean(stream)
        inverse = lax.rsqrt(mean(centre * centre) + epsilon)
        normed = centre * inverse
        sf_d[XH, at, :] = normed
        sf_n[INV, at, :] = spread(inverse)
        normed_b = normed.astype(bf16)
        sb_d[X, at, :] = normed_b
        total = stream
        for c in chunks:
            active, slope, curve = gelu_terms(dot(normed_b, w_up[:, c]))
            active_b = active.astype(bf16)
            sb_f[A, at, c] = active_b
            sf_f[SLOPE, at, c] = slope
            sf_f[CURVE, at, c] = curve
            total = total + dot(active_b, w_down[c, :])
        result = total.astype(bf16)

        if put_up is not None:

            @pl.when(jnp.logical_not(at_last))
            def _():
                put_up[...] = result

        @pl.when(at_last)
        def _():
            gap = result.astype(f32) - goal[at, :].astype(f32)
            sb_d[G, at, :] = (gap * loss_scale).astype(bf16)

    def ready_forward():
        for c in chunks:
            sf_f[XU, :, c] = dot(sb_d[X], u_up[:, c])
        for c in [slice(c, c + CHUNK) for c in range(0, width, CHUNK)]:
            sf_d[AV, :, c] = dot_last(sb_f[A], u_down[c, :])

    def forward_tan(at):
        tangent = got["tan_up"][...].astype(f32)
        tangent = jnp.where(at_first, jnp.zeros_like(tangent), tangent)
        normed = sf_d[XH, at, :]
        inverse = narrow(INV, at)
        centre = tangent - mean(tangent)
        ratio = mean(normed * centre)
        normed_t = inverse * (centre - normed * ratio)
        sf_d[TXF, at, :] = normed_t
        sf_n[RR, at, :] = spread(-inverse * ratio)
        normed_tb = normed_t.astype(bf16)
        sb_d[TX, at, :] = normed_tb
        total = tangent + sf_d[AV, at, :]
        for c in chunks:
            pre_tan = dot(normed_tb, w_up[:, c]) + sf_f[XU, at, c]
            sf_f[TY, at, c] = pre_tan
            active_tb = (sf_f[SLOPE, at, c] * pre_tan).astype(bf16)
            sb_f[TA, at, c] = active_tb
            total = total + dot(active_tb, w_down[c, :])
        result = total.astype(bf16)

        if put_up is not None:

            @pl.when(jnp.logical_not(at_last))
            def _():
                put_up[...] = result

        @pl.when(at_last)
        def _():
            sb_d[TG, at, :] = (result.astype(f32) * loss_scale).astype(bf16)

    def backward(at):
        cotan = jnp.where(at_last, sb_d[G, at, :], got["down"][...])
        sb_d[G, at, :] = cotan
        grad = jnp.zeros((rows, width), f32)
        for c in chunks:
            grad_act = dot_last(cotan, w_down[c, :])
            sf_f[CC, at, c] = grad_act * sf_f[CURVE, at, c]
            grad_pre = (grad_act * sf_f[SLOPE, at, c]).astype(bf16)
            sb_f[PR, at, c] = grad_pre
            grad = grad + dot_last(grad_pre, w_up[:, c])
        sf_d[QN, at, :] = grad
        normed = sf_d[XH, at, :]
        along = mean(grad * normed)
        sf_n[M1, at, :] = spread(along)
        back = narrow(INV, at) * (grad - mean(grad) - normed * along)
        sf_d[BN, at, :] = back
        result = (cotan.astype(f32) + back).astype(bf16)

        if put_down is not None:

            @pl.when(jnp.logical_not(at_first))
            def _():
                put_down[...] = result

    def ready_backward():
        for c in chunks:
            sf_f[GV, :, c] = dot(sb_d[G], u_down[:, c])
        for c in [slice(c, c + CHUNK) for c in range(0, width, CHUNK)]:
            sf_d[PU, :, c] = dot_last(sb_f[PR], u_up[c, :])

    def backward_tan(at):
        cotan_t = jnp.where(at_last, sb_d[TG, at, :], got["tan_down"][...])
        sb_d[TG, at, :] = cotan_t
        grad_t = sf_d[PU, at, :]
        for c in chunks:
            grad_act_t = dot_last(cotan_t, w_down[c, :]) + sf_f[GV, at, c]
            grad_pre_t = grad_act_t * sf_f[SLOPE, at, c] + sf_f[CC, at, c] * sf_f[TY, at, c]
            grad_pre_tb = grad_pre_t.astype(bf16)
            sb_f[TP, at, c] = grad_pre_tb
            grad_t = grad_t + dot_last(grad_pre_tb, w_up[:, c])
        normed, normed_t, inverse = sf_d[XH, at, :], sf_d[TXF, at, :], narrow(INV, at)
        along_t = mean(grad_t * normed + sf_d[QN, at, :] * normed_t)
        inner = grad_t - mean(grad_t) - normed_t * narrow(M1, at) - normed * along_t
        back_t = narrow(RR, at) * sf_d[BN, at, :] + inverse * inner
        result = (cotan_t.astype(f32) + back_t).astype(bf16)

        if put_down is not None:

            @pl.when(jnp.logical_not(at_first))
            def _():
                put_down[...] = result

    if plan.backward_tan(t):
        when_due(t - lag - (2 * layers - 1 - stage), backward_tan)
    if plan.forward_tan(t):
        when_due(t - lag - stage, forward_tan)
    if plan.backward(t):
        when_due(t - (2 * layers - 1 - stage), backward)
    if plan.forward(t):
        when_due(t - stage, forward)
    if plan.ready_forward(t):
        pl.when(stage == t - (lag - 1))(ready_forward)
    if plan.ready_backward(t):
        pl.when(stage == 2 * layers - 2 + lag - t)(ready_backward)


BATCHES = ((4,), (3, 5), (2, 6), (1, 7, 0))


def curvature_kernel(sb_d, sb_f, *refs):
    mine, theirs = refs[: len(BATCHES)], refs[len(BATCHES) : 2 * len(BATCHES)]
    hold = refs[-1]
    hidden = sb_f.shape[2]
    here = lax.axis_index("dp")
    chip, core = here // 2, lax.rem(here, 2)
    chips = lax.axis_size("dp") // 2
    step = hold.shape[0]
    part = step // 2
    for kept, given, batch in zip(mine, theirs, BATCHES):
        for i, far in enumerate(batch):
            at = pl.ds(pl.multiple_of(lax.rem(chip + far, chips) * step, step), step)
            left = jnp.concatenate((sb_d[X, :, at], sb_d[TX, :, at]), axis=0)
            right = jnp.concatenate((sb_f[TP], sb_f[PR]), axis=0)
            hold[:, :hidden] = dot_first(left, right)
            left = jnp.concatenate((sb_d[TG, :, at], sb_d[G, :, at]), axis=0)
            right = jnp.concatenate((sb_f[A], sb_f[TA]), axis=0)
            hold[:, hidden:] = dot_first(left, right)
            kept[i] = hold[pl.ds(pl.multiple_of(core * part, part), part), :].astype(bf16)
            given[i] = hold[pl.ds(pl.multiple_of((1 - core) * part, part), part), :].astype(bf16)


def curvature(sb_d, sb_f, groups):
    width, hidden = sb_d.shape[2], sb_f.shape[2]
    part = width // groups
    parts = tuple(pltpu.VMEM((len(batch), part, 2 * hidden), bf16) for batch in BATCHES)
    outs = pl.pallas_call(
        curvature_kernel,
        out_shape=parts + parts,
        in_specs=[IN_VMEM, IN_VMEM],
        out_specs=(IN_VMEM,) * (2 * len(BATCHES)),
        scratch_shapes=[pltpu.VMEM((2 * part, 2 * hidden), f32)],
        compiler_params=pltpu.CompilerParams(vmem_limit_bytes=12 << 20),
        name="curvature",
    )(vmem(sb_d), vmem(sb_f))
    return outs[: len(BATCHES)], outs[len(BATCHES) :]


def routes(groups):
    return (
        [(i, (i + 2) % groups) for i in range(groups)],
        [(i, (i - 2) % groups) for i in range(groups)],
        [(i, i ^ 1) for i in range(groups)],
    )


def assemble(blocks, halves, groups, part, hidden):
    pieces = [(array, i, (i,), far, other) for array, far, other in blocks for i in range(2)]
    pieces += [(array, i, (), far, other) for array, i, far, other in halves]
    arrays = [b[0] for b in blocks] + [h[0] for h in halves]
    places = [p for p in range(len(blocks)) for _ in range(2)] + [len(blocks) + p for p in range(len(halves))]

    def kernel(*refs):
        sources, targets, sems = refs[: len(arrays)], refs[len(arrays) : -1], refs[-1]
        here = lax.axis_index("dp")
        chip, core = here // 2, lax.rem(here, 2)
        chips = groups // 2
        copies = []
        for n, ((_, probe, index, far, other), place) in enumerate(zip(pieces, places)):
            block = lax.rem(chip + far + chips, chips) * 2 + (1 - core if other else core)
            row = pl.ds(pl.multiple_of(block * part, part), part)
            source = sources[place].at[index] if index else sources[place]
            copies.append(pltpu.make_async_copy(source, targets[probe].at[row, :], sems.at[n]))
        for copy in copies:
            copy.start()
        for copy in copies:
            copy.wait()

    return pl.pallas_call(
        kernel,
        out_shape=tuple(pltpu.VMEM((groups * part, hidden), bf16) for _ in range(2)),
        in_specs=[ANYWHERE] * len(arrays),
        out_specs=(IN_VMEM,) * 2,
        scratch_shapes=[pltpu.SemaphoreType.DMA((len(pieces),))],
        compiler_params=pltpu.CompilerParams(vmem_limit_bytes=1 << 20),
        name="assemble",
    )(*arrays)


def scatter(mine, theirs, groups, hidden):
    ahead, behind, across = routes(groups)

    swapped = []

    def wide(kept, given):
        if swapped:
            given, swapped[-1] = lax.optimization_barrier((given, swapped[-1]))
        swapped.append(lax.ppermute(given, "dp", across))
        return kept.astype(f32) + swapped[-1].astype(f32)

    far = wide(mine[0], theirs[0])[0].astype(bf16)
    from_behind = lax.ppermute(far[:, :hidden], "dp", ahead)
    from_ahead = lax.ppermute(far[:, hidden:], "dp", behind)
    blank_half = ((0, 0), (0, hidden)), ((0, 0), (hidden, 0))
    pair = wide(mine[1], theirs[1])
    up = (pair[0] + jnp.pad(from_behind.astype(f32), blank_half[0])).astype(bf16)
    down = (pair[1] + jnp.pad(from_ahead.astype(f32), blank_half[1])).astype(bf16)
    for kept, given in zip(mine[2:], theirs[2:]):
        from_behind = lax.ppermute(up, "dp", ahead)
        from_ahead = lax.ppermute(down, "dp", behind)
        pair = wide(kept, given)
        up = (pair[0] + from_behind.astype(f32)).astype(bf16)
        down = (pair[1] + from_ahead.astype(f32)).astype(bf16)
    from_behind = lax.ppermute(up, "dp", ahead)
    from_ahead = lax.ppermute(down, "dp", behind)
    return pair[2] + from_behind.astype(f32) + from_ahead.astype(f32)


def on_device(embedded, targets, w_up, w_down, probe_up, probe_down):
    layers = lax.axis_size("pipe")
    groups = lax.axis_size("dp")
    tokens, width = embedded.shape
    hidden = w_up.shape[2]
    part = probe_up.shape[1]
    rows = tokens // PIECES
    loss_scale = 1.0 / (tokens * groups)
    plan = Plan(layers, PIECES, LAG)
    ahead, behind, across = routes(groups)

    swapped = []

    def swap(array):
        if swapped:
            array, swapped[-1] = lax.optimization_barrier((array, swapped[-1]))
        swapped.append(lax.ppermute(array, "dp", across))
        return swapped[-1]

    def ring(both):
        return [lax.ppermute(both[0], "dp", ahead), lax.ppermute(both[1], "dp", behind)]

    own = jnp.stack((probe_up[0], probe_down[0]))
    moving = ring([own, own])
    blocks = [(own, 0, False), (swap(own), 0, True)]
    halves = []

    held = load((w_up[0], w_down[0], embedded, targets))
    *state, nothing = blank(
        (
            ((4, tokens, width), bf16),
            ((4, tokens, hidden), bf16),
            ((6, tokens, width), f32),
            ((6, tokens, hidden), f32),
            ((3, tokens, 128), f32),
            ((rows, width), bf16),
        )
    )
    probes = None
    got = {"up": nothing}
    packet = pltpu.VMEM((rows, width), bf16)
    ring_ticks = {0: 1, 1: 2, 2: 3, 3: 4}
    for t in range(plan.ticks):
        if t == LAG - 1:
            probes = assemble(blocks, halves, groups, part, hidden)
        waves = plan.waves(t)
        ways = [way for way in ("up", "down") if sends(waves, way)]
        with_probes = plan.ready_forward(t) or plan.ready_backward(t)
        operands = list(state) + list(held) + (list(probes) if with_probes else [])
        operands += [got.get(name, nothing) for name in waves]
        outs = pl.pallas_call(
            functools.partial(tick_kernel, plan, t, with_probes, loss_scale, rows, width, hidden),
            out_shape=tuple(pltpu.VMEM(s.shape, s.dtype) for s in state) + (packet,) * len(ways),
            in_specs=[IN_VMEM] * len(operands),
            out_specs=(IN_VMEM,) * (5 + len(ways)),
            input_output_aliases={i: i for i in range(5)},
            compiler_params=pltpu.CompilerParams(vmem_limit_bytes=8 << 20),
            cost_estimate=pl.CostEstimate(flops=1 << 30, bytes_accessed=1 << 23, transcendentals=0),
            name="tick",
        )(*[vmem(o) for o in operands])
        state, sent = outs[:5], dict(zip(ways, outs[5:]))
        got = {
            name: lax.ppermute(sent[name.removeprefix("tan_")], "pipe", edges)
            for name, edges in waves.items()
            if edges
        }
        if t in ring_ticks:
            step = ring_ticks[t]
            got["up"], moving[0], moving[1] = lax.optimization_barrier((got["up"], *moving))
            if step < 4:
                arrived = moving
                moving = ring(arrived if step < 3 else [arrived[0][0], arrived[1][1]])
                for array, away in zip(arrived, (-step, step)):
                    blocks += [(array, away, False), (swap(array), away, True)]
            else:
                for i, array in enumerate(moving):
                    halves += [(array, i, step, False), (swap(array), i, step, True)]

    mine, theirs = curvature(state[0], state[1], groups)
    summed = scatter(mine, theirs, groups, hidden)
    curv_up = probe_up[0].astype(f32) * summed[:, :hidden]
    curv_down = probe_down[0].astype(f32) * summed[:, hidden:]
    return (curv_up[None], curv_down[None])


def solution(mesh):
    in_specs = (
        P("dp", None),
        P("dp", None),
        P("pipe", None, None),
        P("pipe", None, None),
        P("pipe", "dp", None),
        P("pipe", "dp", None),
    )
    out_specs = (P("pipe", "dp", None), P("pipe", "dp", None))
    return jax.shard_map(
        on_device, mesh=mesh, in_specs=in_specs, out_specs=out_specs, check_vma=False
    )
```

```python
import functools

import jax
import jax.numpy as jnp
from jax import lax
from jax.experimental import pallas as pl
from jax.experimental.pallas import tpu as pltpu
from jax.sharding import PartitionSpec as P

PIECES = 4
LAG = 3
CHUNK = 512

epsilon = 1e-05
half_root = 0.7071067811865476
density_scale = 0.3989422804014327

f32 = jnp.float32
bf16 = jnp.bfloat16

X, TX, G, TG = range(4)
A, TA, PR, TP = range(4)
XH, TXF, QN, BN, PU, AV = range(6)
SLOPE, CURVE, TY, XU, CC, GV = range(6)
INV, RR, M1 = range(3)

IN_VMEM = pl.BlockSpec(memory_space=pltpu.VMEM)
ANYWHERE = pl.BlockSpec(memory_space=pl.ANY)


def vmem(array):
    return pltpu.with_memory_space_constraint(array, pltpu.VMEM)


def hbm(array):
    return pltpu.with_memory_space_constraint(array, pltpu.HBM)


def dot(left, right):
    return jnp.dot(left, right, preferred_element_type=f32)


def dot_last(left, right):
    return lax.dot_general(left, right, (((1,), (1,)), ((), ())), preferred_element_type=f32)


def dot_first(left, right):
    return lax.dot_general(left, right, (((0,), (0,)), ((), ())), preferred_element_type=f32)


def mean(values):
    return jnp.mean(values, axis=-1, keepdims=True)


def gelu_terms(values):
    normal_cdf = 0.5 * (1.0 + lax.erf(values * half_root))
    density = density_scale * jnp.exp(-0.5 * values * values)
    return (values * normal_cdf, normal_cdf + values * density, density * (2.0 - values * values))


def load(arrays):
    count = len(arrays)

    def kernel(*refs):
        sources, targets, sems = refs[:count], refs[count : 2 * count], refs[2 * count]
        copies = [
            pltpu.make_async_copy(source, target, sems.at[i])
            for i, (source, target) in enumerate(zip(sources, targets))
        ]
        for copy in copies:
            copy.start()
        for copy in copies:
            copy.wait()

    return pl.pallas_call(
        kernel,
        out_shape=tuple(pltpu.VMEM(a.shape, a.dtype) for a in arrays),
        in_specs=[ANYWHERE] * count,
        out_specs=(IN_VMEM,) * count,
        scratch_shapes=[pltpu.SemaphoreType.DMA((count,))],
        compiler_params=pltpu.CompilerParams(vmem_limit_bytes=1 << 20),
        name="load",
    )(*[hbm(a) for a in arrays])


def blank(shapes):
    def kernel(*refs):
        refs[-1][...] = jnp.zeros(refs[-1].shape, refs[-1].dtype)

    return pl.pallas_call(
        kernel,
        out_shape=tuple(pltpu.VMEM(shape, kind) for shape, kind in shapes),
        out_specs=(IN_VMEM,) * len(shapes),
        compiler_params=pltpu.CompilerParams(vmem_limit_bytes=1 << 20),
        name="blank",
    )()


class Plan:
    def __init__(self, layers, pieces, lag):
        self.layers, self.pieces, self.lag = layers, pieces, lag
        self.ticks = 2 * layers + lag + pieces - 1

    def stages(self, first, step):
        found = [first - step * m for m in range(self.pieces)]
        return [s for s in found if 0 <= s < self.layers]

    def forward(self, t):
        return self.stages(t, 1)

    def forward_tan(self, t):
        return self.stages(t - self.lag, 1)

    def backward(self, t):
        return self.stages(2 * self.layers - 1 - t, -1)

    def backward_tan(self, t):
        return self.stages(2 * self.layers - 1 - t + self.lag, -1)

    def ready_forward(self, t):
        found = [(t - (self.lag - 1) - half * (self.pieces // 2), half) for half in range(2)]
        return [(s, half) for s, half in found if 0 <= s < self.layers]

    def ready_backward(self, t):
        last = 2 * self.layers - 2 + self.lag - t
        found = [(last + half * (self.pieces // 2), half) for half in range(2)]
        return [(s, half) for s, half in found if 0 <= s < self.layers]

    def waves(self, t):
        found = {}
        for name, stages, way in (
            ("tan_up", self.forward_tan(t), 1),
            ("tan_down", self.backward_tan(t), -1),
            ("up", self.forward(t), 1),
            ("down", self.backward(t), -1),
        ):
            if stages:
                useful = [(s, s + way) for s in stages if 0 <= s + way < self.layers]
                if useful == [(self.layers - 2, self.layers - 1)] and self.layers > 2:
                    useful = [(s, s + 1) for s in (self.layers - 2, self.layers - 3)]
                if way < 0 and useful and useful[0][1] == 0:
                    useful = [(s, s - 1) for s in range(1, min(self.pieces + 1, self.layers))]
                found[name] = useful
        return found


def sends(waves, way):
    return bool(waves.get(way)) or bool(waves.get("tan_" + way))


def tick_kernel(plan, t, waves, with_probes, loss_scale, rows, width, hidden, *refs):
    refs = list(refs[5:])
    w_up, w_down, t_up, t_down, source, goal = refs[:6]
    refs = refs[6:]
    if with_probes:
        u_up, u_down = refs[:2]
        refs = refs[2:]
    got = {name: refs.pop(0) for name in waves}
    sb_d, sb_f, sf_d, sf_f, sf_n = refs[:5]
    refs = refs[5:]
    put_up = refs.pop(0) if sends(waves, "up") else None
    put_down = refs.pop(0) if sends(waves, "down") else None

    layers, pieces, lag = plan.layers, plan.pieces, plan.lag
    stage = lax.axis_index("pipe")
    at_first, at_last = stage == 0, stage == layers - 1
    chunks = [slice(c, c + CHUNK) for c in range(0, hidden, CHUNK)]
    lanes = (rows, 128)

    def when_due(piece, work):
        @pl.when((piece >= 0) & (piece < pieces))
        def _():
            work(pl.ds(pl.multiple_of(jnp.clip(piece, 0, pieces - 1) * rows, rows), rows))

    def spread(value):
        return jnp.broadcast_to(value, lanes)

    def narrow(slot, at):
        return sf_n[slot, at, :][:, :1]

    def forward(at):
        stream = jnp.where(at_first, source[at, :], got["up"][...]).astype(f32)
        centre = stream - mean(stream)
        inverse = lax.rsqrt(mean(centre * centre) + epsilon)
        normed = centre * inverse
        sf_d[XH, at, :] = normed
        sf_n[INV, at, :] = spread(inverse)
        normed_b = normed.astype(bf16)
        sb_d[X, at, :] = normed_b
        total = stream
        for c in chunks:
            active, slope, curve = gelu_terms(dot(normed_b, w_up[:, c]))
            active_b = active.astype(bf16)
            sb_f[A, at, c] = active_b
            sf_f[SLOPE, at, c] = slope
            sf_f[CURVE, at, c] = curve
            total = total + dot(active_b, w_down[c, :])
        result = total.astype(bf16)

        if put_up is not None:

            @pl.when(jnp.logical_not(at_last))
            def _():
                put_up[...] = result

        @pl.when(at_last)
        def _():
            gap = result.astype(f32) - goal[at, :].astype(f32)
            sb_d[G, at, :] = (gap * loss_scale).astype(bf16)

    def ready_forward(at):
        for c in chunks:
            sf_f[XU, at, c] = dot(sb_d[X, at, :], u_up[:, c])
        for c in [slice(c, c + CHUNK) for c in range(0, width, CHUNK)]:
            sf_d[AV, at, c] = dot_last(sb_f[A, at, :], u_down[c, :])

    def forward_tan(at):
        tangent = got["tan_up"][...].astype(f32)
        tangent = jnp.where(at_first, jnp.zeros_like(tangent), tangent)
        normed = sf_d[XH, at, :]
        inverse = narrow(INV, at)
        centre = tangent - mean(tangent)
        ratio = mean(normed * centre)
        normed_t = inverse * (centre - normed * ratio)
        sf_d[TXF, at, :] = normed_t
        sf_n[RR, at, :] = spread(-inverse * ratio)
        normed_tb = normed_t.astype(bf16)
        sb_d[TX, at, :] = normed_tb
        total = tangent + sf_d[AV, at, :]
        for c in chunks:
            pre_tan = dot(normed_tb, w_up[:, c]) + sf_f[XU, at, c]
            sf_f[TY, at, c] = pre_tan
            active_tb = (sf_f[SLOPE, at, c] * pre_tan).astype(bf16)
            sb_f[TA, at, c] = active_tb
            total = total + dot(active_tb, w_down[c, :])
        result = total.astype(bf16)

        if put_up is not None:

            @pl.when(jnp.logical_not(at_last))
            def _():
                put_up[...] = result

        @pl.when(at_last)
        def _():
            sb_d[TG, at, :] = (result.astype(f32) * loss_scale).astype(bf16)

    def backward(at):
        cotan = jnp.where(at_last, sb_d[G, at, :], got["down"][...])
        sb_d[G, at, :] = cotan
        grad = jnp.zeros((rows, width), f32)
        for c in chunks:
            grad_act = dot(cotan, t_down[:, c])
            sf_f[CC, at, c] = grad_act * sf_f[CURVE, at, c]
            grad_pre = (grad_act * sf_f[SLOPE, at, c]).astype(bf16)
            sb_f[PR, at, c] = grad_pre
            grad = grad + dot(grad_pre, t_up[c, :])
        sf_d[QN, at, :] = grad
        normed = sf_d[XH, at, :]
        along = mean(grad * normed)
        sf_n[M1, at, :] = spread(along)
        back = narrow(INV, at) * (grad - mean(grad) - normed * along)
        sf_d[BN, at, :] = back
        result = (cotan.astype(f32) + back).astype(bf16)

        if put_down is not None:

            @pl.when(jnp.logical_not(at_first))
            def _():
                put_down[...] = result

    def ready_backward(at):
        for c in chunks:
            sf_f[GV, at, c] = dot(sb_d[G, at, :], u_down[:, c])
        for c in [slice(c, c + CHUNK) for c in range(0, width, CHUNK)]:
            sf_d[PU, at, c] = dot_last(sb_f[PR, at, :], u_up[c, :])

    def backward_tan(at):
        cotan_t = jnp.where(at_last, sb_d[TG, at, :], got["tan_down"][...])
        sb_d[TG, at, :] = cotan_t
        grad_t = sf_d[PU, at, :]
        for c in chunks:
            grad_act_t = dot(cotan_t, t_down[:, c]) + sf_f[GV, at, c]
            grad_pre_t = grad_act_t * sf_f[SLOPE, at, c] + sf_f[CC, at, c] * sf_f[TY, at, c]
            grad_pre_tb = grad_pre_t.astype(bf16)
            sb_f[TP, at, c] = grad_pre_tb
            grad_t = grad_t + dot(grad_pre_tb, t_up[c, :])
        normed, normed_t, inverse = sf_d[XH, at, :], sf_d[TXF, at, :], narrow(INV, at)
        along_t = mean(grad_t * normed + sf_d[QN, at, :] * normed_t)
        inner = grad_t - mean(grad_t) - normed_t * narrow(M1, at) - normed * along_t
        back_t = narrow(RR, at) * sf_d[BN, at, :] + inverse * inner
        result = (cotan_t.astype(f32) + back_t).astype(bf16)

        if put_down is not None:

            @pl.when(jnp.logical_not(at_first))
            def _():
                put_down[...] = result

    if "tan_down" in waves:
        when_due(t - lag - (2 * layers - 1 - stage), backward_tan)
    if "tan_up" in waves:
        when_due(t - lag - stage, forward_tan)
    if "down" in waves:
        when_due(t - (2 * layers - 1 - stage), backward)
    if "up" in waves:
        when_due(t - stage, forward)
    if with_probes:
        group = pieces // 2 * rows
        for due, work in ((plan.ready_forward(t), ready_forward), (plan.ready_backward(t), ready_backward)):
            for layer, half in due:
                at = slice(half * group, (half + 1) * group)
                pl.when(stage == layer)(functools.partial(work, at))


def transposed(arrays):
    count = len(arrays)

    def kernel(*refs):
        for source, target in zip(refs[:count], refs[count:]):
            for c in range(0, source.shape[0], 256):
                target[:, c : c + 256] = source[c : c + 256, :].T

    return pl.pallas_call(
        kernel,
        out_shape=tuple(pltpu.VMEM(a.shape[::-1], a.dtype) for a in arrays),
        in_specs=[IN_VMEM] * count,
        out_specs=(IN_VMEM,) * count,
        compiler_params=pltpu.CompilerParams(vmem_limit_bytes=4 << 20),
        cost_estimate=pl.CostEstimate(flops=1 << 30, bytes_accessed=1 << 24, transcendentals=0),
        name="transposed",
    )(*[vmem(a) for a in arrays])


BATCHES = ((4,), (3, 5), (2, 6), (1, 7, 0))


def curvature_kernel(sb_d, sb_f, *refs):
    mine, theirs = refs[: len(BATCHES)], refs[len(BATCHES) : 2 * len(BATCHES)]
    hold = refs[-1]
    hidden = sb_f.shape[2]
    here = lax.axis_index("dp")
    chip, core = here // 2, lax.rem(here, 2)
    chips = lax.axis_size("dp") // 2
    step = hold.shape[0]
    part = step // 2
    for kept, given, batch in zip(mine, theirs, BATCHES):
        for i, far in enumerate(batch):
            at = pl.ds(pl.multiple_of(lax.rem(chip + far, chips) * step, step), step)
            left = jnp.concatenate((sb_d[X, :, at], sb_d[TX, :, at]), axis=0)
            right = jnp.concatenate((sb_f[TP], sb_f[PR]), axis=0)
            hold[:, :hidden] = dot_first(left, right)
            left = jnp.concatenate((sb_d[TG, :, at], sb_d[G, :, at]), axis=0)
            right = jnp.concatenate((sb_f[A], sb_f[TA]), axis=0)
            hold[:, hidden:] = dot_first(left, right)
            kept[i] = hold[pl.ds(pl.multiple_of(core * part, part), part), :].astype(bf16)
            given[i] = hold[pl.ds(pl.multiple_of((1 - core) * part, part), part), :].astype(bf16)


def curvature(sb_d, sb_f, groups):
    width, hidden = sb_d.shape[2], sb_f.shape[2]
    part = width // groups
    parts = tuple(pltpu.VMEM((len(batch), part, 2 * hidden), bf16) for batch in BATCHES)
    outs = pl.pallas_call(
        curvature_kernel,
        out_shape=parts + parts,
        in_specs=[IN_VMEM, IN_VMEM],
        out_specs=(IN_VMEM,) * (2 * len(BATCHES)),
        scratch_shapes=[pltpu.VMEM((2 * part, 2 * hidden), f32)],
        compiler_params=pltpu.CompilerParams(vmem_limit_bytes=12 << 20),
        name="curvature",
    )(vmem(sb_d), vmem(sb_f))
    return outs[: len(BATCHES)], outs[len(BATCHES) :]


def routes(groups):
    return (
        [(i, (i + 2) % groups) for i in range(groups)],
        [(i, (i - 2) % groups) for i in range(groups)],
        [(i, i ^ 1) for i in range(groups)],
    )


def assemble(blocks, halves, groups, part, hidden):
    pieces = [(array, i, (i,), far, other) for array, far, other in blocks for i in range(2)]
    pieces += [(array, i, (), far, other) for array, i, far, other in halves]
    arrays = [b[0] for b in blocks] + [h[0] for h in halves]
    places = [p for p in range(len(blocks)) for _ in range(2)] + [len(blocks) + p for p in range(len(halves))]

    def kernel(*refs):
        sources, targets, sems = refs[: len(arrays)], refs[len(arrays) : -1], refs[-1]
        here = lax.axis_index("dp")
        chip, core = here // 2, lax.rem(here, 2)
        chips = groups // 2
        copies = []
        for n, ((_, probe, index, far, other), place) in enumerate(zip(pieces, places)):
            block = lax.rem(chip + far + chips, chips) * 2 + (1 - core if other else core)
            row = pl.ds(pl.multiple_of(block * part, part), part)
            source = sources[place].at[index] if index else sources[place]
            copies.append(pltpu.make_async_copy(source, targets[probe].at[row, :], sems.at[n]))
        for copy in copies:
            copy.start()
        for copy in copies:
            copy.wait()

    return pl.pallas_call(
        kernel,
        out_shape=tuple(pltpu.VMEM((groups * part, hidden), bf16) for _ in range(2)),
        in_specs=[ANYWHERE] * len(arrays),
        out_specs=(IN_VMEM,) * 2,
        scratch_shapes=[pltpu.SemaphoreType.DMA((len(pieces),))],
        compiler_params=pltpu.CompilerParams(vmem_limit_bytes=1 << 20),
        name="assemble",
    )(*arrays)


def scatter(mine, theirs, groups, hidden):
    ahead, behind, across = routes(groups)

    swapped = []

    def wide(kept, given):
        if swapped:
            given, swapped[-1] = lax.optimization_barrier((given, swapped[-1]))
        swapped.append(lax.ppermute(given, "dp", across))
        return kept.astype(f32) + swapped[-1].astype(f32)

    far = wide(mine[0], theirs[0])[0].astype(bf16)
    from_behind = lax.ppermute(far[:, :hidden], "dp", ahead)
    from_ahead = lax.ppermute(far[:, hidden:], "dp", behind)
    blank_half = ((0, 0), (0, hidden)), ((0, 0), (hidden, 0))
    pair = wide(mine[1], theirs[1])
    up = (pair[0] + jnp.pad(from_behind.astype(f32), blank_half[0])).astype(bf16)
    down = (pair[1] + jnp.pad(from_ahead.astype(f32), blank_half[1])).astype(bf16)
    for kept, given in zip(mine[2:], theirs[2:]):
        from_behind = lax.ppermute(up, "dp", ahead)
        from_ahead = lax.ppermute(down, "dp", behind)
        pair = wide(kept, given)
        up = (pair[0] + from_behind.astype(f32)).astype(bf16)
        down = (pair[1] + from_ahead.astype(f32)).astype(bf16)
    from_behind = lax.ppermute(up, "dp", ahead)
    from_ahead = lax.ppermute(down, "dp", behind)
    return pair[2] + from_behind.astype(f32) + from_ahead.astype(f32)


def on_device(embedded, targets, w_up, w_down, probe_up, probe_down):
    layers = lax.axis_size("pipe")
    groups = lax.axis_size("dp")
    tokens, width = embedded.shape
    hidden = w_up.shape[2]
    part = probe_up.shape[1]
    rows = tokens // PIECES
    loss_scale = 1.0 / (tokens * groups)
    plan = Plan(layers, PIECES, LAG)
    ahead, behind, across = routes(groups)

    swapped = []

    def swap(array):
        if swapped:
            array, swapped[-1] = lax.optimization_barrier((array, swapped[-1]))
        swapped.append(lax.ppermute(array, "dp", across))
        return swapped[-1]

    def ring(both):
        return [lax.ppermute(both[0], "dp", ahead), lax.ppermute(both[1], "dp", behind)]

    own = jnp.stack((probe_up[0], probe_down[0]))
    moving = ring([own, own])
    blocks = [(own, 0, False), (swap(own), 0, True)]
    halves = []

    weights, ends = [], load((w_up[0], w_down[0], embedded, targets))
    weights, ends = list(ends[:2]), list(ends[2:])
    turned = weights
    *state, nothing = blank(
        (
            ((4, tokens, width), bf16),
            ((4, tokens, hidden), bf16),
            ((6, tokens, width), f32),
            ((6, tokens, hidden), f32),
            ((3, tokens, 128), f32),
            ((rows, width), bf16),
        )
    )
    probes = None
    got = {"up": nothing}
    packet = pltpu.VMEM((rows, width), bf16)

    def keep(arrived, step):
        for array, away in zip(arrived, (-step, step)):
            blocks.extend([(array, away, False), (swap(array), away, True)])

    def part_of_tick(t, waves, with_probes, got, state):
        ways = [way for way in ("up", "down") if sends(waves, way)]
        operands = list(state) + weights + list(turned) + ends + (list(probes) if with_probes else [])
        operands += [got.get(name, nothing) for name in waves]
        outs = pl.pallas_call(
            functools.partial(tick_kernel, plan, t, waves, with_probes, loss_scale, rows, width, hidden),
            out_shape=tuple(pltpu.VMEM(s.shape, s.dtype) for s in state) + (packet,) * len(ways),
            in_specs=[IN_VMEM] * len(operands),
            out_specs=(IN_VMEM,) * (5 + len(ways)),
            input_output_aliases={i: i for i in range(5)},
            compiler_params=pltpu.CompilerParams(vmem_limit_bytes=8 << 20),
            cost_estimate=pl.CostEstimate(flops=1 << 30, bytes_accessed=1 << 23, transcendentals=0),
            name="tick",
        )(*[vmem(o) for o in operands])
        state, sent = outs[:5], dict(zip(ways, outs[5:]))
        arrived = {
            name: lax.ppermute(sent[name.removeprefix("tan_")], "pipe", edges)
            for name, edges in waves.items()
            if edges
        }
        return state, arrived

    for t in range(plan.ticks):
        waves = plan.waves(t)
        arrived = {}
        ready = bool(plan.ready_forward(t) or plan.ready_backward(t))
        leading = {name: edges for name, edges in waves.items() if name.startswith("tan_")}
        following = {name: edges for name, edges in waves.items() if name not in leading}
        if leading:
            state, more = part_of_tick(t, leading, False, got, state)
            arrived.update(more)
        if following or ready:
            state, more = part_of_tick(t, following, ready, got, state)
            arrived.update(more)
        got = arrived
        if t == 0:
            got["up"], *moving = lax.optimization_barrier((got["up"], *moving))
            moved, moving = moving, ring(moving)
            keep(moved, 1)
        if t == 1:
            got["up"], *moving = lax.optimization_barrier((got["up"], *moving))
            moved, moving = moving, ring(moving)
            keep(moved, 2)
            weights[0], moved[0] = lax.optimization_barrier((weights[0], moved[0]))
            turned = transposed(weights)
            *turned, moving[0], moving[1] = lax.optimization_barrier((*turned, *moving))
            moved, moving = moving, ring([moving[0][0], moving[1][1]])
            keep(moved, 3)
            for i, array in enumerate(moving):
                halves += [(array, i, 4, False), (swap(array), i, 4, True)]
            probes = assemble(blocks, halves, groups, part, hidden)

    mine, theirs = curvature(state[0], state[1], groups)
    summed = scatter(mine, theirs, groups, hidden)
    curv_up = probe_up[0].astype(f32) * summed[:, :hidden]
    curv_down = probe_down[0].astype(f32) * summed[:, hidden:]
    return (curv_up[None], curv_down[None])


def solution(mesh):
    in_specs = (
        P("dp", None),
        P("dp", None),
        P("pipe", None, None),
        P("pipe", None, None),
        P("pipe", "dp", None),
        P("pipe", "dp", None),
    )
    out_specs = (P("pipe", "dp", None), P("pipe", "dp", None))
    return jax.shard_map(
        on_device, mesh=mesh, in_specs=in_specs, out_specs=out_specs, check_vma=False
    )
```

```python
import functools

import jax
import jax.numpy as jnp
from jax import lax
from jax.experimental import pallas as pl
from jax.experimental.pallas import tpu as pltpu
from jax.sharding import PartitionSpec as P

PIECES = 4
LAG = 7
CHUNK = 512

epsilon = 1e-05
half_root = 0.7071067811865476
density_scale = 0.3989422804014327

f32 = jnp.float32
bf16 = jnp.bfloat16

X, TX, G, TG = range(4)
A, TA, PR, TP = range(4)
XH, TXF, QN, BN, PU, AV = range(6)
SLOPE, CURVE, TY, XU, CC, GV = range(6)
INV, RR, M1 = range(3)

IN_VMEM = pl.BlockSpec(memory_space=pltpu.VMEM)
ANYWHERE = pl.BlockSpec(memory_space=pl.ANY)


def vmem(array):
    return pltpu.with_memory_space_constraint(array, pltpu.VMEM)


def hbm(array):
    return pltpu.with_memory_space_constraint(array, pltpu.HBM)


def dot(left, right):
    return jnp.dot(left, right, preferred_element_type=f32)


def dot_last(left, right):
    return lax.dot_general(left, right, (((1,), (1,)), ((), ())), preferred_element_type=f32)


def dot_first(left, right):
    return lax.dot_general(left, right, (((0,), (0,)), ((), ())), preferred_element_type=f32)


def mean(values):
    return jnp.mean(values, axis=-1, keepdims=True)


def gelu_terms(values):
    normal_cdf = 0.5 * (1.0 + lax.erf(values * half_root))
    density = density_scale * jnp.exp(-0.5 * values * values)
    return (values * normal_cdf, normal_cdf + values * density, density * (2.0 - values * values))


def load(arrays):
    count = len(arrays)

    def kernel(*refs):
        sources, targets, sems = refs[:count], refs[count : 2 * count], refs[2 * count]
        copies = [
            pltpu.make_async_copy(source, target, sems.at[i])
            for i, (source, target) in enumerate(zip(sources, targets))
        ]
        for copy in copies:
            copy.start()
        for copy in copies:
            copy.wait()

    return pl.pallas_call(
        kernel,
        out_shape=tuple(pltpu.VMEM(a.shape, a.dtype) for a in arrays),
        in_specs=[ANYWHERE] * count,
        out_specs=(IN_VMEM,) * count,
        scratch_shapes=[pltpu.SemaphoreType.DMA((count,))],
        compiler_params=pltpu.CompilerParams(vmem_limit_bytes=1 << 20),
        name="load",
    )(*[hbm(a) for a in arrays])


def blank(shapes):
    def kernel(*refs):
        refs[-1][...] = jnp.zeros(refs[-1].shape, refs[-1].dtype)

    return pl.pallas_call(
        kernel,
        out_shape=tuple(pltpu.VMEM(shape, kind) for shape, kind in shapes),
        out_specs=(IN_VMEM,) * len(shapes),
        compiler_params=pltpu.CompilerParams(vmem_limit_bytes=1 << 20),
        name="blank",
    )()


class Plan:
    def __init__(self, layers, pieces, lag):
        self.layers, self.pieces, self.lag = layers, pieces, lag
        self.ticks = 2 * layers + lag + pieces - 1

    def stages(self, first, step):
        found = [first - step * m for m in range(self.pieces)]
        return [s for s in found if 0 <= s < self.layers]

    def forward(self, t):
        return self.stages(t, 1)

    def forward_tan(self, t):
        return self.stages(t - self.lag, 1)

    def backward(self, t):
        return self.stages(2 * self.layers - 1 - t, -1)

    def backward_tan(self, t):
        return self.stages(2 * self.layers - 1 - t + self.lag, -1)

    def ready_forward(self, t):
        found = [(t - (self.lag - 1) - half * (self.pieces // 2), half) for half in range(2)]
        return [(s, half) for s, half in found if 0 <= s < self.layers]

    def ready_backward(self, t):
        last = 2 * self.layers - 2 + self.lag - t
        found = [(last + half * (self.pieces // 2), half) for half in range(2)]
        return [(s, half) for s, half in found if 0 <= s < self.layers]

    def waves(self, t):
        found = {}
        for name, stages, way in (
            ("tan_up", self.forward_tan(t), 1),
            ("tan_down", self.backward_tan(t), -1),
            ("up", self.forward(t), 1),
            ("down", self.backward(t), -1),
        ):
            if stages:
                useful = [(s, s + way) for s in stages if 0 <= s + way < self.layers]
                if useful == [(self.layers - 2, self.layers - 1)] and self.layers > 2:
                    useful = [(s, s + 1) for s in (self.layers - 2, self.layers - 3)]
                if way < 0 and useful and useful[0][1] == 0:
                    useful = [(s, s - 1) for s in range(1, min(self.pieces + 1, self.layers))]
                found[name] = useful
        return found


def sends(waves, way):
    return bool(waves.get(way)) or bool(waves.get("tan_" + way))


def tick_kernel(plan, t, waves, with_probes, loss_scale, rows, width, hidden, *refs):
    refs = list(refs[5:])
    w_up, w_down, t_up, t_down, source, goal = refs[:6]
    refs = refs[6:]
    if with_probes:
        u_up, u_down = refs[:2]
        refs = refs[2:]
    got = {name: refs.pop(0) for name in waves}
    sb_d, sb_f, sf_d, sf_f, sf_n = refs[:5]
    refs = refs[5:]
    put_up = refs.pop(0) if sends(waves, "up") else None
    put_down = refs.pop(0) if sends(waves, "down") else None

    layers, pieces, lag = plan.layers, plan.pieces, plan.lag
    stage = lax.axis_index("pipe")
    at_first, at_last = stage == 0, stage == layers - 1
    chunks = [slice(c, c + CHUNK) for c in range(0, hidden, CHUNK)]
    lanes = (rows, 128)

    def when_due(piece, work):
        @pl.when((piece >= 0) & (piece < pieces))
        def _():
            work(pl.ds(pl.multiple_of(jnp.clip(piece, 0, pieces - 1) * rows, rows), rows))

    def spread(value):
        return jnp.broadcast_to(value, lanes)

    def narrow(slot, at):
        return sf_n[slot, at, :][:, :1]

    def forward(at):
        stream = jnp.where(at_first, source[at, :], got["up"][...]).astype(f32)
        centre = stream - mean(stream)
        inverse = lax.rsqrt(mean(centre * centre) + epsilon)
        normed = centre * inverse
        sf_d[XH, at, :] = normed
        sf_n[INV, at, :] = spread(inverse)
        normed_b = normed.astype(bf16)
        sb_d[X, at, :] = normed_b
        total = stream
        for c in chunks:
            active, slope, curve = gelu_terms(dot(normed_b, w_up[:, c]))
            active_b = active.astype(bf16)
            sb_f[A, at, c] = active_b
            sf_f[SLOPE, at, c] = slope
            sf_f[CURVE, at, c] = curve
            total = total + dot(active_b, w_down[c, :])
        result = total.astype(bf16)

        if put_up is not None:

            @pl.when(jnp.logical_not(at_last))
            def _():
                put_up[...] = result

        @pl.when(at_last)
        def _():
            gap = result.astype(f32) - goal[at, :].astype(f32)
            sb_d[G, at, :] = (gap * loss_scale).astype(bf16)

    def ready_forward(at):
        for c in chunks:
            sf_f[XU, at, c] = dot(sb_d[X, at, :], u_up[:, c])
        for c in [slice(c, c + CHUNK) for c in range(0, width, CHUNK)]:
            sf_d[AV, at, c] = dot_last(sb_f[A, at, :], u_down[c, :])

    def forward_tan(at):
        tangent = got["tan_up"][...].astype(f32)
        tangent = jnp.where(at_first, jnp.zeros_like(tangent), tangent)
        normed = sf_d[XH, at, :]
        inverse = narrow(INV, at)
        centre = tangent - mean(tangent)
        ratio = mean(normed * centre)
        normed_t = inverse * (centre - normed * ratio)
        sf_d[TXF, at, :] = normed_t
        sf_n[RR, at, :] = spread(-inverse * ratio)
        normed_tb = normed_t.astype(bf16)
        sb_d[TX, at, :] = normed_tb
        total = tangent + sf_d[AV, at, :]
        for c in chunks:
            pre_tan = dot(normed_tb, w_up[:, c]) + sf_f[XU, at, c]
            sf_f[TY, at, c] = pre_tan
            active_tb = (sf_f[SLOPE, at, c] * pre_tan).astype(bf16)
            sb_f[TA, at, c] = active_tb
            total = total + dot(active_tb, w_down[c, :])
        result = total.astype(bf16)

        if put_up is not None:

            @pl.when(jnp.logical_not(at_last))
            def _():
                put_up[...] = result

        @pl.when(at_last)
        def _():
            sb_d[TG, at, :] = (result.astype(f32) * loss_scale).astype(bf16)

    def backward(at):
        cotan = jnp.where(at_last, sb_d[G, at, :], got["down"][...])
        sb_d[G, at, :] = cotan
        grad = jnp.zeros((rows, width), f32)
        for c in chunks:
            grad_act = dot(cotan, t_down[:, c])
            sf_f[CC, at, c] = grad_act * sf_f[CURVE, at, c]
            grad_pre = (grad_act * sf_f[SLOPE, at, c]).astype(bf16)
            sb_f[PR, at, c] = grad_pre
            grad = grad + dot(grad_pre, t_up[c, :])
        sf_d[QN, at, :] = grad
        normed = sf_d[XH, at, :]
        along = mean(grad * normed)
        sf_n[M1, at, :] = spread(along)
        back = narrow(INV, at) * (grad - mean(grad) - normed * along)
        sf_d[BN, at, :] = back
        result = (cotan.astype(f32) + back).astype(bf16)

        if put_down is not None:

            @pl.when(jnp.logical_not(at_first))
            def _():
                put_down[...] = result

    def ready_backward(at):
        for c in chunks:
            sf_f[GV, at, c] = dot(sb_d[G, at, :], u_down[:, c])
        for c in [slice(c, c + CHUNK) for c in range(0, width, CHUNK)]:
            sf_d[PU, at, c] = dot_last(sb_f[PR, at, :], u_up[c, :])

    def backward_tan(at):
        cotan_t = jnp.where(at_last, sb_d[TG, at, :], got["tan_down"][...])
        sb_d[TG, at, :] = cotan_t
        grad_t = sf_d[PU, at, :]
        for c in chunks:
            grad_act_t = dot(cotan_t, t_down[:, c]) + sf_f[GV, at, c]
            grad_pre_t = grad_act_t * sf_f[SLOPE, at, c] + sf_f[CC, at, c] * sf_f[TY, at, c]
            grad_pre_tb = grad_pre_t.astype(bf16)
            sb_f[TP, at, c] = grad_pre_tb
            grad_t = grad_t + dot(grad_pre_tb, t_up[c, :])
        normed, normed_t, inverse = sf_d[XH, at, :], sf_d[TXF, at, :], narrow(INV, at)
        along_t = mean(grad_t * normed + sf_d[QN, at, :] * normed_t)
        inner = grad_t - mean(grad_t) - normed_t * narrow(M1, at) - normed * along_t
        back_t = narrow(RR, at) * sf_d[BN, at, :] + inverse * inner
        result = (cotan_t.astype(f32) + back_t).astype(bf16)

        if put_down is not None:

            @pl.when(jnp.logical_not(at_first))
            def _():
                put_down[...] = result

    if "tan_down" in waves:
        when_due(t - lag - (2 * layers - 1 - stage), backward_tan)
    if "tan_up" in waves:
        when_due(t - lag - stage, forward_tan)
    if "down" in waves:
        when_due(t - (2 * layers - 1 - stage), backward)
    if "up" in waves:
        when_due(t - stage, forward)
    if with_probes:
        group = pieces // 2 * rows
        for due, work in ((plan.ready_forward(t), ready_forward), (plan.ready_backward(t), ready_backward)):
            for layer, half in due:
                at = slice(half * group, (half + 1) * group)
                pl.when(stage == layer)(functools.partial(work, at))


def transposed(arrays):
    count = len(arrays)

    def kernel(*refs):
        for source, target in zip(refs[:count], refs[count:]):
            for c in range(0, source.shape[0], 256):
                target[:, c : c + 256] = source[c : c + 256, :].T

    return pl.pallas_call(
        kernel,
        out_shape=tuple(pltpu.VMEM(a.shape[::-1], a.dtype) for a in arrays),
        in_specs=[IN_VMEM] * count,
        out_specs=(IN_VMEM,) * count,
        compiler_params=pltpu.CompilerParams(vmem_limit_bytes=4 << 20),
        cost_estimate=pl.CostEstimate(flops=1 << 30, bytes_accessed=1 << 24, transcendentals=0),
        name="transposed",
    )(*[vmem(a) for a in arrays])


BATCHES = ((4,), (3, 5), (2, 6), (1, 7, 0))


def curvature_kernel(sb_d, sb_f, *refs):
    mine, theirs = refs[: len(BATCHES)], refs[len(BATCHES) : 2 * len(BATCHES)]
    hold = refs[-1]
    hidden = sb_f.shape[2]
    here = lax.axis_index("dp")
    chip, core = here // 2, lax.rem(here, 2)
    chips = lax.axis_size("dp") // 2
    step = hold.shape[0]
    part = step // 2
    for kept, given, batch in zip(mine, theirs, BATCHES):
        for i, far in enumerate(batch):
            at = pl.ds(pl.multiple_of(lax.rem(chip + far, chips) * step, step), step)
            left = jnp.concatenate((sb_d[X, :, at], sb_d[TX, :, at]), axis=0)
            right = jnp.concatenate((sb_f[TP], sb_f[PR]), axis=0)
            hold[:, :hidden] = dot_first(left, right)
            left = jnp.concatenate((sb_d[TG, :, at], sb_d[G, :, at]), axis=0)
            right = jnp.concatenate((sb_f[A], sb_f[TA]), axis=0)
            hold[:, hidden:] = dot_first(left, right)
            kept[i] = hold[pl.ds(pl.multiple_of(core * part, part), part), :].astype(bf16)
            given[i] = hold[pl.ds(pl.multiple_of((1 - core) * part, part), part), :].astype(bf16)


def curvature(sb_d, sb_f, groups):
    width, hidden = sb_d.shape[2], sb_f.shape[2]
    part = width // groups
    parts = tuple(pltpu.VMEM((len(batch), part, 2 * hidden), bf16) for batch in BATCHES)
    outs = pl.pallas_call(
        curvature_kernel,
        out_shape=parts + parts,
        in_specs=[IN_VMEM, IN_VMEM],
        out_specs=(IN_VMEM,) * (2 * len(BATCHES)),
        scratch_shapes=[pltpu.VMEM((2 * part, 2 * hidden), f32)],
        compiler_params=pltpu.CompilerParams(vmem_limit_bytes=12 << 20),
        name="curvature",
    )(vmem(sb_d), vmem(sb_f))
    return outs[: len(BATCHES)], outs[len(BATCHES) :]


def routes(groups):
    return (
        [(i, (i + 2) % groups) for i in range(groups)],
        [(i, (i - 2) % groups) for i in range(groups)],
        [(i, i ^ 1) for i in range(groups)],
    )


def assemble(blocks, halves, groups, part, hidden):
    pieces = [(array, i, (i,), far, other) for array, far, other in blocks for i in range(2)]
    pieces += [(array, i, (), far, other) for array, i, far, other in halves]
    arrays = [b[0] for b in blocks] + [h[0] for h in halves]
    places = [p for p in range(len(blocks)) for _ in range(2)] + [len(blocks) + p for p in range(len(halves))]

    def kernel(*refs):
        sources, targets, sems = refs[: len(arrays)], refs[len(arrays) : -1], refs[-1]
        here = lax.axis_index("dp")
        chip, core = here // 2, lax.rem(here, 2)
        chips = groups // 2
        copies = []
        for n, ((_, probe, index, far, other), place) in enumerate(zip(pieces, places)):
            block = lax.rem(chip + far + chips, chips) * 2 + (1 - core if other else core)
            row = pl.ds(pl.multiple_of(block * part, part), part)
            source = sources[place].at[index] if index else sources[place]
            copies.append(pltpu.make_async_copy(source, targets[probe].at[row, :], sems.at[n]))
        for copy in copies:
            copy.start()
        for copy in copies:
            copy.wait()

    return pl.pallas_call(
        kernel,
        out_shape=tuple(pltpu.VMEM((groups * part, hidden), bf16) for _ in range(2)),
        in_specs=[ANYWHERE] * len(arrays),
        out_specs=(IN_VMEM,) * 2,
        scratch_shapes=[pltpu.SemaphoreType.DMA((len(pieces),))],
        compiler_params=pltpu.CompilerParams(vmem_limit_bytes=1 << 20),
        name="assemble",
    )(*arrays)


def scatter(mine, theirs, groups, hidden):
    ahead, behind, across = routes(groups)

    swapped = []

    def wide(kept, given):
        if swapped:
            given, swapped[-1] = lax.optimization_barrier((given, swapped[-1]))
        swapped.append(lax.ppermute(given, "dp", across))
        return kept.astype(f32) + swapped[-1].astype(f32)

    far = wide(mine[0], theirs[0])[0].astype(bf16)
    from_behind = lax.ppermute(far[:, :hidden], "dp", ahead)
    from_ahead = lax.ppermute(far[:, hidden:], "dp", behind)
    blank_half = ((0, 0), (0, hidden)), ((0, 0), (hidden, 0))
    pair = wide(mine[1], theirs[1])
    up = (pair[0] + jnp.pad(from_behind.astype(f32), blank_half[0])).astype(bf16)
    down = (pair[1] + jnp.pad(from_ahead.astype(f32), blank_half[1])).astype(bf16)
    for kept, given in zip(mine[2:], theirs[2:]):
        from_behind = lax.ppermute(up, "dp", ahead)
        from_ahead = lax.ppermute(down, "dp", behind)
        pair = wide(kept, given)
        up = (pair[0] + from_behind.astype(f32)).astype(bf16)
        down = (pair[1] + from_ahead.astype(f32)).astype(bf16)
    from_behind = lax.ppermute(up, "dp", ahead)
    from_ahead = lax.ppermute(down, "dp", behind)
    return pair[2] + from_behind.astype(f32) + from_ahead.astype(f32)


def on_device(embedded, targets, w_up, w_down, probe_up, probe_down):
    layers = lax.axis_size("pipe")
    groups = lax.axis_size("dp")
    tokens, width = embedded.shape
    hidden = w_up.shape[2]
    part = probe_up.shape[1]
    rows = tokens // PIECES
    loss_scale = 1.0 / (tokens * groups)
    plan = Plan(layers, PIECES, LAG)
    ahead, behind, across = routes(groups)

    swapped = []

    def swap(array):
        if swapped:
            array, swapped[-1] = lax.optimization_barrier((array, swapped[-1]))
        swapped.append(lax.ppermute(array, "dp", across))
        return swapped[-1]

    def ring(both):
        return [lax.ppermute(both[0], "dp", ahead), lax.ppermute(both[1], "dp", behind)]

    own = jnp.stack((probe_up[0], probe_down[0]))
    moving = ring([own, own])
    blocks = [(own, 0, False), (swap(own), 0, True)]
    halves = []

    weights, ends = [], load((w_up[0], w_down[0], embedded, targets))
    weights, ends = list(ends[:2]), list(ends[2:])
    turned = weights
    *state, nothing = blank(
        (
            ((4, tokens, width), bf16),
            ((4, tokens, hidden), bf16),
            ((6, tokens, width), f32),
            ((6, tokens, hidden), f32),
            ((3, tokens, 128), f32),
            ((rows, width), bf16),
        )
    )
    probes = None
    got = {"up": nothing}
    packet = pltpu.VMEM((rows, width), bf16)

    def keep(arrived, step):
        for array, away in zip(arrived, (-step, step)):
            blocks.extend([(array, away, False), (swap(array), away, True)])

    def part_of_tick(t, waves, with_probes, got, state):
        ways = [way for way in ("up", "down") if sends(waves, way)]
        operands = list(state) + weights + list(turned) + ends + (list(probes) if with_probes else [])
        operands += [got.get(name, nothing) for name in waves]
        outs = pl.pallas_call(
            functools.partial(tick_kernel, plan, t, waves, with_probes, loss_scale, rows, width, hidden),
            out_shape=tuple(pltpu.VMEM(s.shape, s.dtype) for s in state) + (packet,) * len(ways),
            in_specs=[IN_VMEM] * len(operands),
            out_specs=(IN_VMEM,) * (5 + len(ways)),
            input_output_aliases={i: i for i in range(5)},
            compiler_params=pltpu.CompilerParams(vmem_limit_bytes=8 << 20),
            cost_estimate=pl.CostEstimate(flops=1 << 30, bytes_accessed=1 << 23, transcendentals=0),
            name="tick",
        )(*[vmem(o) for o in operands])
        state, sent = outs[:5], dict(zip(ways, outs[5:]))
        arrived = {
            name: lax.ppermute(sent[name.removeprefix("tan_")], "pipe", edges)
            for name, edges in waves.items()
            if edges
        }
        return state, arrived

    for t in range(plan.ticks):
        waves = plan.waves(t)
        arrived = {}
        ready = bool(plan.ready_forward(t) or plan.ready_backward(t))
        leading = {name: edges for name, edges in waves.items() if name.startswith("tan_")}
        following = {name: edges for name, edges in waves.items() if name not in leading}
        if leading:
            state, more = part_of_tick(t, leading, False, got, state)
            arrived.update(more)
        if following or ready:
            state, more = part_of_tick(t, following, ready, got, state)
            arrived.update(more)
        got = arrived
        if t <= 3:
            got["up"], *moving = lax.optimization_barrier((got["up"], *moving))
            moved = moving
            if t < 3:
                moving = ring(moved if t < 2 else [moved[0][0], moved[1][1]])
                keep(moved, t + 1)
            else:
                for i, array in enumerate(moved):
                    halves += [(array, i, 4, False), (swap(array), i, 4, True)]
                weights[0], got["up"] = lax.optimization_barrier((weights[0], got["up"]))
                turned = transposed(weights)
        if t == LAG - 2:
            probes = assemble(blocks, halves, groups, part, hidden)

    mine, theirs = curvature(state[0], state[1], groups)
    summed = scatter(mine, theirs, groups, hidden)
    curv_up = probe_up[0].astype(f32) * summed[:, :hidden]
    curv_down = probe_down[0].astype(f32) * summed[:, hidden:]
    return (curv_up[None], curv_down[None])


def solution(mesh):
    in_specs = (
        P("dp", None),
        P("dp", None),
        P("pipe", None, None),
        P("pipe", None, None),
        P("pipe", "dp", None),
        P("pipe", "dp", None),
    )
    out_specs = (P("pipe", "dp", None), P("pipe", "dp", None))
    return jax.shard_map(
        on_device, mesh=mesh, in_specs=in_specs, out_specs=out_specs, check_vma=False
    )
```

```python
import functools

import jax
import jax.numpy as jnp
from jax import lax
from jax.experimental import pallas as pl
from jax.experimental.pallas import tpu as pltpu
from jax.sharding import PartitionSpec as P

PIECES = 4
LAG = 7
TURN = 2
CHUNK = 512

epsilon = 1e-05
half_root = 0.7071067811865476
density_scale = 0.3989422804014327

f32 = jnp.float32
bf16 = jnp.bfloat16

X, TX, G, TG = range(4)
A, TA, PR, TP = range(4)
XH, TXF, QN, BN, PU, AV = range(6)
SLOPE, CURVE, TY, XU, CC, GV = range(6)
INV, RR, M1 = range(3)

IN_VMEM = pl.BlockSpec(memory_space=pltpu.VMEM)
ANYWHERE = pl.BlockSpec(memory_space=pl.ANY)


def vmem(array):
    return pltpu.with_memory_space_constraint(array, pltpu.VMEM)


def hbm(array):
    return pltpu.with_memory_space_constraint(array, pltpu.HBM)


def dot(left, right):
    return jnp.dot(left, right, preferred_element_type=f32)


def dot_last(left, right):
    return lax.dot_general(left, right, (((1,), (1,)), ((), ())), preferred_element_type=f32)


def dot_first(left, right):
    return lax.dot_general(left, right, (((0,), (0,)), ((), ())), preferred_element_type=f32)


def mean(values):
    return jnp.mean(values, axis=-1, keepdims=True)


def gelu_terms(values):
    normal_cdf = 0.5 * (1.0 + lax.erf(values * half_root))
    density = density_scale * jnp.exp(-0.5 * values * values)
    return (values * normal_cdf, normal_cdf + values * density, density * (2.0 - values * values))


def load(arrays):
    count = len(arrays)

    def kernel(*refs):
        sources, targets, sems = refs[:count], refs[count : 2 * count], refs[2 * count]
        copies = [
            pltpu.make_async_copy(source, target, sems.at[i])
            for i, (source, target) in enumerate(zip(sources, targets))
        ]
        for copy in copies:
            copy.start()
        for copy in copies:
            copy.wait()

    return pl.pallas_call(
        kernel,
        out_shape=tuple(pltpu.VMEM(a.shape, a.dtype) for a in arrays),
        in_specs=[ANYWHERE] * count,
        out_specs=(IN_VMEM,) * count,
        scratch_shapes=[pltpu.SemaphoreType.DMA((count,))],
        compiler_params=pltpu.CompilerParams(vmem_limit_bytes=1 << 20),
        name="load",
    )(*[hbm(a) for a in arrays])


def blank(shapes):
    def kernel(*refs):
        refs[-1][...] = jnp.zeros(refs[-1].shape, refs[-1].dtype)

    return pl.pallas_call(
        kernel,
        out_shape=tuple(pltpu.VMEM(shape, kind) for shape, kind in shapes),
        out_specs=(IN_VMEM,) * len(shapes),
        compiler_params=pltpu.CompilerParams(vmem_limit_bytes=1 << 20),
        name="blank",
    )()


class Plan:
    def __init__(self, layers, pieces, lag):
        self.layers, self.pieces, self.lag = layers, pieces, lag
        self.ticks = 2 * layers + lag + pieces - 1

    def stages(self, first, step):
        found = [first - step * m for m in range(self.pieces)]
        return [s for s in found if 0 <= s < self.layers]

    def forward(self, t):
        return self.stages(t, 1)

    def forward_tan(self, t):
        return self.stages(t - self.lag, 1)

    def backward(self, t):
        return self.stages(2 * self.layers - 1 + TURN - t, -1)

    def backward_tan(self, t):
        return self.stages(2 * self.layers - 1 - t + self.lag, -1)

    def ready_forward(self, t):
        found = [(t - (self.lag - 1) - half * (self.pieces // 2), half) for half in range(2)]
        return [(s, half) for s, half in found if 0 <= s < self.layers]

    def ready_backward(self, t):
        last = 2 * self.layers - 2 + self.lag - t
        found = [(last + half * (self.pieces // 2), half) for half in range(2)]
        return [(s, half) for s, half in found if 0 <= s < self.layers]

    def waves(self, t):
        found = {}
        for name, stages, way in (
            ("tan_up", self.forward_tan(t), 1),
            ("tan_down", self.backward_tan(t), -1),
            ("up", self.forward(t), 1),
            ("down", self.backward(t), -1),
        ):
            if stages:
                useful = [(s, s + way) for s in stages if 0 <= s + way < self.layers]
                if useful == [(self.layers - 2, self.layers - 1)] and self.layers > 2:
                    useful = [(s, s + 1) for s in (self.layers - 2, self.layers - 3)]
                if way < 0 and useful and useful[0][1] == 0:
                    useful = [(s, s - 1) for s in range(1, min(self.pieces + 1, self.layers))]
                found[name] = useful
        return found


def sends(waves, way):
    return bool(waves.get(way)) or bool(waves.get("tan_" + way))


def tick_kernel(plan, t, waves, with_probes, loss_scale, rows, width, hidden, *refs):
    refs = list(refs[5:])
    w_up, w_down, t_up, t_down, source, goal = refs[:6]
    refs = refs[6:]
    if with_probes:
        u_up, u_down = refs[:2]
        refs = refs[2:]
    got = {name: refs.pop(0) for name in waves}
    sb_d, sb_f, sf_d, sf_f, sf_n = refs[:5]
    refs = refs[5:]
    put_up = refs.pop(0) if sends(waves, "up") else None
    put_down = refs.pop(0) if sends(waves, "down") else None

    layers, pieces, lag = plan.layers, plan.pieces, plan.lag
    stage = lax.axis_index("pipe")
    at_first, at_last = stage == 0, stage == layers - 1
    chunks = [slice(c, c + CHUNK) for c in range(0, hidden, CHUNK)]
    lanes = (rows, 128)

    def when_due(piece, work):
        @pl.when((piece >= 0) & (piece < pieces))
        def _():
            work(pl.ds(pl.multiple_of(jnp.clip(piece, 0, pieces - 1) * rows, rows), rows))

    def spread(value):
        return jnp.broadcast_to(value, lanes)

    def narrow(slot, at):
        return sf_n[slot, at, :][:, :1]

    def forward(at):
        stream = jnp.where(at_first, source[at, :], got["up"][...]).astype(f32)
        centre = stream - mean(stream)
        inverse = lax.rsqrt(mean(centre * centre) + epsilon)
        normed = centre * inverse
        sf_d[XH, at, :] = normed
        sf_n[INV, at, :] = spread(inverse)
        normed_b = normed.astype(bf16)
        sb_d[X, at, :] = normed_b
        total = stream
        for c in chunks:
            active, slope, curve = gelu_terms(dot(normed_b, w_up[:, c]))
            active_b = active.astype(bf16)
            sb_f[A, at, c] = active_b
            sf_f[SLOPE, at, c] = slope
            sf_f[CURVE, at, c] = curve
            total = total + dot(active_b, w_down[c, :])
        result = total.astype(bf16)

        if put_up is not None:

            @pl.when(jnp.logical_not(at_last))
            def _():
                put_up[...] = result

        @pl.when(at_last)
        def _():
            gap = result.astype(f32) - goal[at, :].astype(f32)
            sb_d[G, at, :] = (gap * loss_scale).astype(bf16)

    def ready_forward(at):
        for c in chunks:
            sf_f[XU, at, c] = dot(sb_d[X, at, :], u_up[:, c])
        for c in [slice(c, c + CHUNK) for c in range(0, width, CHUNK)]:
            sf_d[AV, at, c] = dot_last(sb_f[A, at, :], u_down[c, :])

    def forward_tan(at):
        tangent = got["tan_up"][...].astype(f32)
        tangent = jnp.where(at_first, jnp.zeros_like(tangent), tangent)
        normed = sf_d[XH, at, :]
        inverse = narrow(INV, at)
        centre = tangent - mean(tangent)
        ratio = mean(normed * centre)
        normed_t = inverse * (centre - normed * ratio)
        sf_d[TXF, at, :] = normed_t
        sf_n[RR, at, :] = spread(-inverse * ratio)
        normed_tb = normed_t.astype(bf16)
        sb_d[TX, at, :] = normed_tb
        total = tangent + sf_d[AV, at, :]
        for c in chunks:
            pre_tan = dot(normed_tb, w_up[:, c]) + sf_f[XU, at, c]
            sf_f[TY, at, c] = pre_tan
            active_tb = (sf_f[SLOPE, at, c] * pre_tan).astype(bf16)
            sb_f[TA, at, c] = active_tb
            total = total + dot(active_tb, w_down[c, :])
        result = total.astype(bf16)

        if put_up is not None:

            @pl.when(jnp.logical_not(at_last))
            def _():
                put_up[...] = result

        @pl.when(at_last)
        def _():
            sb_d[TG, at, :] = (result.astype(f32) * loss_scale).astype(bf16)

    def backward(at):
        cotan = jnp.where(at_last, sb_d[G, at, :], got["down"][...])
        sb_d[G, at, :] = cotan
        grad = jnp.zeros((rows, width), f32)
        for c in chunks:
            grad_act = dot(cotan, t_down[:, c])
            sf_f[CC, at, c] = grad_act * sf_f[CURVE, at, c]
            grad_pre = (grad_act * sf_f[SLOPE, at, c]).astype(bf16)
            sb_f[PR, at, c] = grad_pre
            grad = grad + dot(grad_pre, t_up[c, :])
        sf_d[QN, at, :] = grad
        normed = sf_d[XH, at, :]
        along = mean(grad * normed)
        sf_n[M1, at, :] = spread(along)
        back = narrow(INV, at) * (grad - mean(grad) - normed * along)
        sf_d[BN, at, :] = back
        result = (cotan.astype(f32) + back).astype(bf16)

        if put_down is not None:

            @pl.when(jnp.logical_not(at_first))
            def _():
                put_down[...] = result

    def ready_backward(at):
        for c in chunks:
            sf_f[GV, at, c] = dot(sb_d[G, at, :], u_down[:, c])
        for c in [slice(c, c + CHUNK) for c in range(0, width, CHUNK)]:
            sf_d[PU, at, c] = dot_last(sb_f[PR, at, :], u_up[c, :])

    def backward_tan(at):
        cotan_t = jnp.where(at_last, sb_d[TG, at, :], got["tan_down"][...])
        sb_d[TG, at, :] = cotan_t
        grad_t = sf_d[PU, at, :]
        for c in chunks:
            grad_act_t = dot(cotan_t, t_down[:, c]) + sf_f[GV, at, c]
            grad_pre_t = grad_act_t * sf_f[SLOPE, at, c] + sf_f[CC, at, c] * sf_f[TY, at, c]
            grad_pre_tb = grad_pre_t.astype(bf16)
            sb_f[TP, at, c] = grad_pre_tb
            grad_t = grad_t + dot(grad_pre_tb, t_up[c, :])
        normed, normed_t, inverse = sf_d[XH, at, :], sf_d[TXF, at, :], narrow(INV, at)
        along_t = mean(grad_t * normed + sf_d[QN, at, :] * normed_t)
        inner = grad_t - mean(grad_t) - normed_t * narrow(M1, at) - normed * along_t
        back_t = narrow(RR, at) * sf_d[BN, at, :] + inverse * inner
        result = (cotan_t.astype(f32) + back_t).astype(bf16)

        if put_down is not None:

            @pl.when(jnp.logical_not(at_first))
            def _():
                put_down[...] = result

    if "tan_down" in waves:
        when_due(t - lag - (2 * layers - 1 - stage), backward_tan)
    if "tan_up" in waves:
        when_due(t - lag - stage, forward_tan)
    if "down" in waves:
        when_due(t - TURN - (2 * layers - 1 - stage), backward)
    if "up" in waves:
        when_due(t - stage, forward)
    if with_probes:
        group = pieces // 2 * rows
        for due, work in ((plan.ready_forward(t), ready_forward), (plan.ready_backward(t), ready_backward)):
            for layer, half in due:
                at = slice(half * group, (half + 1) * group)
                pl.when(stage == layer)(functools.partial(work, at))


def transposed(arrays):
    count = len(arrays)

    def kernel(*refs):
        for source, target in zip(refs[:count], refs[count:]):
            for c in range(0, source.shape[0], 256):
                target[:, c : c + 256] = source[c : c + 256, :].T

    return pl.pallas_call(
        kernel,
        out_shape=tuple(pltpu.VMEM(a.shape[::-1], a.dtype) for a in arrays),
        in_specs=[IN_VMEM] * count,
        out_specs=(IN_VMEM,) * count,
        compiler_params=pltpu.CompilerParams(vmem_limit_bytes=4 << 20),
        cost_estimate=pl.CostEstimate(flops=1 << 30, bytes_accessed=1 << 24, transcendentals=0),
        name="transposed",
    )(*[vmem(a) for a in arrays])


BATCHES = ((4,), (3, 5), (2, 6), (1, 7, 0))


def curvature_kernel(batches, sb_d, sb_f, *refs):
    mine, theirs = refs[: len(batches)], refs[len(batches) : 2 * len(batches)]
    hold = refs[-1]
    hidden = sb_f.shape[2]
    here = lax.axis_index("dp")
    chip, core = here // 2, lax.rem(here, 2)
    chips = lax.axis_size("dp") // 2
    step = hold.shape[0]
    part = step // 2
    for kept, given, batch in zip(mine, theirs, batches):
        for i, far in enumerate(batch):
            at = pl.ds(pl.multiple_of(lax.rem(chip + far, chips) * step, step), step)
            left = jnp.concatenate((sb_d[X, :, at], sb_d[TX, :, at]), axis=0)
            right = jnp.concatenate((sb_f[TP], sb_f[PR]), axis=0)
            hold[:, :hidden] = dot_first(left, right)
            left = jnp.concatenate((sb_d[TG, :, at], sb_d[G, :, at]), axis=0)
            right = jnp.concatenate((sb_f[A], sb_f[TA]), axis=0)
            hold[:, hidden:] = dot_first(left, right)
            kept[i] = hold[pl.ds(pl.multiple_of(core * part, part), part), :].astype(bf16)
            given[i] = hold[pl.ds(pl.multiple_of((1 - core) * part, part), part), :].astype(bf16)


def curvature(sb_d, sb_f, groups, batches):
    width, hidden = sb_d.shape[2], sb_f.shape[2]
    part = width // groups
    parts = tuple(pltpu.VMEM((len(batch), part, 2 * hidden), bf16) for batch in batches)
    outs = pl.pallas_call(
        functools.partial(curvature_kernel, batches),
        out_shape=parts + parts,
        in_specs=[IN_VMEM, IN_VMEM],
        out_specs=(IN_VMEM,) * (2 * len(batches)),
        scratch_shapes=[pltpu.VMEM((2 * part, 2 * hidden), f32)],
        compiler_params=pltpu.CompilerParams(vmem_limit_bytes=12 << 20),
        cost_estimate=pl.CostEstimate(flops=1 << 31, bytes_accessed=1 << 23, transcendentals=0),
        name="curvature",
    )(vmem(sb_d), vmem(sb_f))
    return outs[: len(batches)], outs[len(batches) :]


def routes(groups):
    return (
        [(i, (i + 2) % groups) for i in range(groups)],
        [(i, (i - 2) % groups) for i in range(groups)],
        [(i, i ^ 1) for i in range(groups)],
    )


def assemble(blocks, halves, groups, part, hidden):
    pieces = [(array, i, (i,), far, other) for array, far, other in blocks for i in range(2)]
    pieces += [(array, i, (), far, other) for array, i, far, other in halves]
    arrays = [b[0] for b in blocks] + [h[0] for h in halves]
    places = [p for p in range(len(blocks)) for _ in range(2)] + [len(blocks) + p for p in range(len(halves))]

    def kernel(*refs):
        sources, targets, sems = refs[: len(arrays)], refs[len(arrays) : -1], refs[-1]
        here = lax.axis_index("dp")
        chip, core = here // 2, lax.rem(here, 2)
        chips = groups // 2
        copies = []
        for n, ((_, probe, index, far, other), place) in enumerate(zip(pieces, places)):
            block = lax.rem(chip + far + chips, chips) * 2 + (1 - core if other else core)
            row = pl.ds(pl.multiple_of(block * part, part), part)
            source = sources[place].at[index] if index else sources[place]
            copies.append(pltpu.make_async_copy(source, targets[probe].at[row, :], sems.at[n]))
        for copy in copies:
            copy.start()
        for copy in copies:
            copy.wait()

    return pl.pallas_call(
        kernel,
        out_shape=tuple(pltpu.VMEM((groups * part, hidden), bf16) for _ in range(2)),
        in_specs=[ANYWHERE] * len(arrays),
        out_specs=(IN_VMEM,) * 2,
        scratch_shapes=[pltpu.SemaphoreType.DMA((len(pieces),))],
        compiler_params=pltpu.CompilerParams(vmem_limit_bytes=1 << 20),
        name="assemble",
    )(*arrays)


def scatter(mine, theirs, groups, hidden):
    ahead, behind, across = routes(groups)

    swapped = []

    def wide(kept, given):
        if swapped:
            given, swapped[-1] = lax.optimization_barrier((given, swapped[-1]))
        swapped.append(lax.ppermute(given, "dp", across))
        return kept.astype(f32) + swapped[-1].astype(f32)

    far = wide(mine[0], theirs[0])[0].astype(bf16)
    from_behind = lax.ppermute(far[:, :hidden], "dp", ahead)
    from_ahead = lax.ppermute(far[:, hidden:], "dp", behind)
    blank_half = ((0, 0), (0, hidden)), ((0, 0), (hidden, 0))
    pair = wide(mine[1], theirs[1])
    up = (pair[0] + jnp.pad(from_behind.astype(f32), blank_half[0])).astype(bf16)
    down = (pair[1] + jnp.pad(from_ahead.astype(f32), blank_half[1])).astype(bf16)
    for kept, given in zip(mine[2:], theirs[2:]):
        from_behind = lax.ppermute(up, "dp", ahead)
        from_ahead = lax.ppermute(down, "dp", behind)
        pair = wide(kept, given)
        up = (pair[0] + from_behind.astype(f32)).astype(bf16)
        down = (pair[1] + from_ahead.astype(f32)).astype(bf16)
    from_behind = lax.ppermute(up, "dp", ahead)
    from_ahead = lax.ppermute(down, "dp", behind)
    return pair[2] + from_behind.astype(f32) + from_ahead.astype(f32)


def on_device(embedded, targets, w_up, w_down, probe_up, probe_down):
    layers = lax.axis_size("pipe")
    groups = lax.axis_size("dp")
    tokens, width = embedded.shape
    hidden = w_up.shape[2]
    part = probe_up.shape[1]
    rows = tokens // PIECES
    loss_scale = 1.0 / (tokens * groups)
    plan = Plan(layers, PIECES, LAG)
    ahead, behind, across = routes(groups)

    swapped = []

    def swap(array):
        if swapped:
            array, swapped[-1] = lax.optimization_barrier((array, swapped[-1]))
        swapped.append(lax.ppermute(array, "dp", across))
        return swapped[-1]

    def ring(both):
        return [lax.ppermute(both[0], "dp", ahead), lax.ppermute(both[1], "dp", behind)]

    own = jnp.stack((probe_up[0], probe_down[0]))
    moving = ring([own, own])
    blocks = [(own, 0, False), (swap(own), 0, True)]
    halves = []

    weights, ends = [], load((w_up[0], w_down[0], embedded, targets))
    weights, ends = list(ends[:2]), list(ends[2:])
    turned = weights
    *state, nothing = blank(
        (
            ((4, tokens, width), bf16),
            ((4, tokens, hidden), bf16),
            ((6, tokens, width), f32),
            ((6, tokens, hidden), f32),
            ((3, tokens, 128), f32),
            ((rows, width), bf16),
        )
    )
    probes = None
    got = {"up": nothing}
    packet = pltpu.VMEM((rows, width), bf16)

    def keep(arrived, step):
        for array, away in zip(arrived, (-step, step)):
            blocks.extend([(array, away, False), (swap(array), away, True)])

    def part_of_tick(t, waves, with_probes, got, state):
        ways = [way for way in ("up", "down") if sends(waves, way)]
        operands = list(state) + weights + list(turned) + ends + (list(probes) if with_probes else [])
        operands += [got.get(name, nothing) for name in waves]
        outs = pl.pallas_call(
            functools.partial(tick_kernel, plan, t, waves, with_probes, loss_scale, rows, width, hidden),
            out_shape=tuple(pltpu.VMEM(s.shape, s.dtype) for s in state) + (packet,) * len(ways),
            in_specs=[IN_VMEM] * len(operands),
            out_specs=(IN_VMEM,) * (5 + len(ways)),
            input_output_aliases={i: i for i in range(5)},
            compiler_params=pltpu.CompilerParams(vmem_limit_bytes=8 << 20),
            cost_estimate=pl.CostEstimate(flops=1 << 30, bytes_accessed=1 << 23, transcendentals=0),
            name="tick",
        )(*[vmem(o) for o in operands])
        state, sent = outs[:5], dict(zip(ways, outs[5:]))
        arrived = {
            name: lax.ppermute(sent[name.removeprefix("tan_")], "pipe", edges)
            for name, edges in waves.items()
            if edges
        }
        return state, arrived

    for t in range(plan.ticks):
        waves = plan.waves(t)
        arrived = {}
        ready = bool(plan.ready_forward(t) or plan.ready_backward(t))
        following = {name: edges for name, edges in waves.items() if not name.startswith("tan_")}
        for name in ("tan_down", "tan_up"):
            if name in waves:
                state, more = part_of_tick(t, {name: waves[name]}, False, got, state)
                arrived.update(more)
        if following or ready:
            state, more = part_of_tick(t, following, ready, got, state)
            arrived.update(more)
        got = arrived
        if t <= 3:
            got["up"], *moving = lax.optimization_barrier((got["up"], *moving))
            moved = moving
            if t < 3:
                moving = ring(moved if t < 2 else [moved[0][0], moved[1][1]])
                keep(moved, t + 1)
            else:
                for i, array in enumerate(moved):
                    halves += [(array, i, 4, False), (swap(array), i, 4, True)]
                weights[0], got["up"] = lax.optimization_barrier((weights[0], got["up"]))
                turned = transposed(weights)
        if t == LAG - 2:
            probes = assemble(blocks, halves, groups, part, hidden)

    mine, theirs = (), ()
    for batches in (BATCHES[:1], BATCHES[1:]):
        kept, given = curvature(state[0], state[1], groups, batches)
        mine, theirs = mine + tuple(kept), theirs + tuple(given)
    summed = scatter(mine, theirs, groups, hidden)
    curv_up = probe_up[0].astype(f32) * summed[:, :hidden]
    curv_down = probe_down[0].astype(f32) * summed[:, hidden:]
    return (curv_up[None], curv_down[None])


def solution(mesh):
    in_specs = (
        P("dp", None),
        P("dp", None),
        P("pipe", None, None),
        P("pipe", None, None),
        P("pipe", "dp", None),
        P("pipe", "dp", None),
    )
    out_specs = (P("pipe", "dp", None), P("pipe", "dp", None))
    return jax.shard_map(
        on_device, mesh=mesh, in_specs=in_specs, out_specs=out_specs, check_vma=False
    )
```

```python
import functools

import jax
import jax.numpy as jnp
from jax import lax
from jax.experimental import pallas as pl
from jax.experimental.pallas import tpu as pltpu
from jax.sharding import PartitionSpec as P

PIECES = 4
LAG = 7
TURN = 1
CHUNK = 512

epsilon = 1e-05
half_root = 0.7071067811865476
density_scale = 0.3989422804014327

f32 = jnp.float32
bf16 = jnp.bfloat16

X, TX, G, TG = range(4)
A, TA, PR, TP = range(4)
XH, TXF, QN, BN, PU, AV = range(6)
SLOPE, CURVE, TY, XU, CC, GV = range(6)
INV, RR, M1 = range(3)

IN_VMEM = pl.BlockSpec(memory_space=pltpu.VMEM)
ANYWHERE = pl.BlockSpec(memory_space=pl.ANY)


def vmem(array):
    return pltpu.with_memory_space_constraint(array, pltpu.VMEM)


def hbm(array):
    return pltpu.with_memory_space_constraint(array, pltpu.HBM)


def dot(left, right):
    return jnp.dot(left, right, preferred_element_type=f32)


def dot_last(left, right):
    return lax.dot_general(left, right, (((1,), (1,)), ((), ())), preferred_element_type=f32)


def dot_first(left, right):
    return lax.dot_general(left, right, (((0,), (0,)), ((), ())), preferred_element_type=f32)


def mean(values):
    return jnp.mean(values, axis=-1, keepdims=True)


def gelu_terms(values):
    normal_cdf = 0.5 * (1.0 + lax.erf(values * half_root))
    density = density_scale * jnp.exp(-0.5 * values * values)
    return (values * normal_cdf, normal_cdf + values * density, density * (2.0 - values * values))


def load(arrays):
    count = len(arrays)

    def kernel(*refs):
        sources, targets, sems = refs[:count], refs[count : 2 * count], refs[2 * count]
        copies = [
            pltpu.make_async_copy(source, target, sems.at[i])
            for i, (source, target) in enumerate(zip(sources, targets))
        ]
        for copy in copies:
            copy.start()
        for copy in copies:
            copy.wait()

    return pl.pallas_call(
        kernel,
        out_shape=tuple(pltpu.VMEM(a.shape, a.dtype) for a in arrays),
        in_specs=[ANYWHERE] * count,
        out_specs=(IN_VMEM,) * count,
        scratch_shapes=[pltpu.SemaphoreType.DMA((count,))],
        compiler_params=pltpu.CompilerParams(vmem_limit_bytes=1 << 20),
        name="load",
    )(*[hbm(a) for a in arrays])


def blank(shapes):
    def kernel(*refs):
        refs[-1][...] = jnp.zeros(refs[-1].shape, refs[-1].dtype)

    return pl.pallas_call(
        kernel,
        out_shape=tuple(pltpu.VMEM(shape, kind) for shape, kind in shapes),
        out_specs=(IN_VMEM,) * len(shapes),
        compiler_params=pltpu.CompilerParams(vmem_limit_bytes=1 << 20),
        name="blank",
    )()


class Plan:
    def __init__(self, layers, pieces, lag):
        self.layers, self.pieces, self.lag = layers, pieces, lag
        self.ticks = 2 * layers + lag + pieces - 1

    def stages(self, first, step):
        found = [first - step * m for m in range(self.pieces)]
        return [s for s in found if 0 <= s < self.layers]

    def forward(self, t):
        return self.stages(t, 1)

    def forward_tan(self, t):
        return self.stages(t - self.lag, 1)

    def backward(self, t):
        return self.stages(2 * self.layers - 1 + TURN - t, -1)

    def backward_tan(self, t):
        return self.stages(2 * self.layers - 1 - t + self.lag, -1)

    def ready_forward(self, t):
        found = [(t - (self.lag - 1) - half * (self.pieces // 2), half) for half in range(2)]
        return [(s, half) for s, half in found if 0 <= s < self.layers]

    def ready_backward(self, t):
        last = 2 * self.layers - 2 + self.lag - t
        found = [(last + half * (self.pieces // 2), half) for half in range(2)]
        return [(s, half) for s, half in found if 0 <= s < self.layers]

    def waves(self, t):
        found = {}
        for name, stages, way in (
            ("tan_up", self.forward_tan(t), 1),
            ("tan_down", self.backward_tan(t), -1),
            ("up", self.forward(t), 1),
            ("down", self.backward(t), -1),
        ):
            if stages:
                useful = [(s, s + way) for s in stages if 0 <= s + way < self.layers]
                if useful == [(self.layers - 2, self.layers - 1)] and self.layers > 2:
                    useful = [(s, s + 1) for s in (self.layers - 2, self.layers - 3)]
                if way < 0 and useful and useful[0][1] == 0:
                    useful = [(s, s - 1) for s in range(1, min(self.pieces + 1, self.layers))]
                found[name] = useful
        return found


def sends(waves, way):
    return bool(waves.get(way)) or bool(waves.get("tan_" + way))


def tick_kernel(plan, t, waves, with_probes, loss_scale, rows, width, hidden, *refs):
    refs = list(refs[5:])
    w_up, w_down, t_up, t_down, source, goal = refs[:6]
    refs = refs[6:]
    if with_probes:
        u_up, u_down = refs[:2]
        refs = refs[2:]
    got = {name: refs.pop(0) for name in waves}
    sb_d, sb_f, sf_d, sf_f, sf_n = refs[:5]
    refs = refs[5:]
    put_up = refs.pop(0) if sends(waves, "up") else None
    put_down = refs.pop(0) if sends(waves, "down") else None

    layers, pieces, lag = plan.layers, plan.pieces, plan.lag
    stage = lax.axis_index("pipe")
    at_first, at_last = stage == 0, stage == layers - 1
    chunks = [slice(c, c + CHUNK) for c in range(0, hidden, CHUNK)]
    lanes = (rows, 128)

    def when_due(piece, work):
        @pl.when((piece >= 0) & (piece < pieces))
        def _():
            work(pl.ds(pl.multiple_of(jnp.clip(piece, 0, pieces - 1) * rows, rows), rows))

    def spread(value):
        return jnp.broadcast_to(value, lanes)

    def narrow(slot, at):
        return sf_n[slot, at, :][:, :1]

    def forward(at):
        stream = jnp.where(at_first, source[at, :], got["up"][...]).astype(f32)
        centre = stream - mean(stream)
        inverse = lax.rsqrt(mean(centre * centre) + epsilon)
        normed = centre * inverse
        sf_d[XH, at, :] = normed
        sf_n[INV, at, :] = spread(inverse)
        normed_b = normed.astype(bf16)
        sb_d[X, at, :] = normed_b
        total = stream
        for c in chunks:
            active, slope, curve = gelu_terms(dot(normed_b, w_up[:, c]))
            active_b = active.astype(bf16)
            sb_f[A, at, c] = active_b
            sf_f[SLOPE, at, c] = slope
            sf_f[CURVE, at, c] = curve
            total = total + dot(active_b, w_down[c, :])
        result = total.astype(bf16)

        if put_up is not None:

            @pl.when(jnp.logical_not(at_last))
            def _():
                put_up[...] = result

        @pl.when(at_last)
        def _():
            gap = result.astype(f32) - goal[at, :].astype(f32)
            sb_d[G, at, :] = (gap * loss_scale).astype(bf16)

    def ready_forward(at):
        for c in chunks:
            sf_f[XU, at, c] = dot(sb_d[X, at, :], u_up[:, c])
        for c in [slice(c, c + CHUNK) for c in range(0, width, CHUNK)]:
            sf_d[AV, at, c] = dot_last(sb_f[A, at, :], u_down[c, :])

    def forward_tan(at):
        tangent = got["tan_up"][...].astype(f32)
        tangent = jnp.where(at_first, jnp.zeros_like(tangent), tangent)
        normed = sf_d[XH, at, :]
        inverse = narrow(INV, at)
        centre = tangent - mean(tangent)
        ratio = mean(normed * centre)
        normed_t = inverse * (centre - normed * ratio)
        sf_d[TXF, at, :] = normed_t
        sf_n[RR, at, :] = spread(-inverse * ratio)
        normed_tb = normed_t.astype(bf16)
        sb_d[TX, at, :] = normed_tb
        total = tangent + sf_d[AV, at, :]
        for c in chunks:
            pre_tan = dot(normed_tb, w_up[:, c]) + sf_f[XU, at, c]
            sf_f[TY, at, c] = pre_tan
            active_tb = (sf_f[SLOPE, at, c] * pre_tan).astype(bf16)
            sb_f[TA, at, c] = active_tb
            total = total + dot(active_tb, w_down[c, :])
        result = total.astype(bf16)

        if put_up is not None:

            @pl.when(jnp.logical_not(at_last))
            def _():
                put_up[...] = result

        @pl.when(at_last)
        def _():
            sb_d[TG, at, :] = (result.astype(f32) * loss_scale).astype(bf16)

    def backward(at):
        cotan = jnp.where(at_last, sb_d[G, at, :], got["down"][...])
        sb_d[G, at, :] = cotan
        grad = jnp.zeros((rows, width), f32)
        for c in chunks:
            grad_act = dot(cotan, t_down[:, c])
            sf_f[CC, at, c] = grad_act * sf_f[CURVE, at, c]
            grad_pre = (grad_act * sf_f[SLOPE, at, c]).astype(bf16)
            sb_f[PR, at, c] = grad_pre
            grad = grad + dot(grad_pre, t_up[c, :])
        sf_d[QN, at, :] = grad
        normed = sf_d[XH, at, :]
        along = mean(grad * normed)
        sf_n[M1, at, :] = spread(along)
        back = narrow(INV, at) * (grad - mean(grad) - normed * along)
        sf_d[BN, at, :] = back
        result = (cotan.astype(f32) + back).astype(bf16)

        if put_down is not None:

            @pl.when(jnp.logical_not(at_first))
            def _():
                put_down[...] = result

    def ready_backward(at):
        for c in chunks:
            sf_f[GV, at, c] = dot(sb_d[G, at, :], u_down[:, c])
        for c in [slice(c, c + CHUNK) for c in range(0, width, CHUNK)]:
            sf_d[PU, at, c] = dot_last(sb_f[PR, at, :], u_up[c, :])

    def backward_tan(at):
        cotan_t = jnp.where(at_last, sb_d[TG, at, :], got["tan_down"][...])
        sb_d[TG, at, :] = cotan_t
        grad_t = sf_d[PU, at, :]
        for c in chunks:
            grad_act_t = dot(cotan_t, t_down[:, c]) + sf_f[GV, at, c]
            grad_pre_t = grad_act_t * sf_f[SLOPE, at, c] + sf_f[CC, at, c] * sf_f[TY, at, c]
            grad_pre_tb = grad_pre_t.astype(bf16)
            sb_f[TP, at, c] = grad_pre_tb
            grad_t = grad_t + dot(grad_pre_tb, t_up[c, :])
        normed, normed_t, inverse = sf_d[XH, at, :], sf_d[TXF, at, :], narrow(INV, at)
        along_t = mean(grad_t * normed + sf_d[QN, at, :] * normed_t)
        inner = grad_t - mean(grad_t) - normed_t * narrow(M1, at) - normed * along_t
        back_t = narrow(RR, at) * sf_d[BN, at, :] + inverse * inner
        result = (cotan_t.astype(f32) + back_t).astype(bf16)

        if put_down is not None:

            @pl.when(jnp.logical_not(at_first))
            def _():
                put_down[...] = result

    if "tan_down" in waves:
        when_due(t - lag - (2 * layers - 1 - stage), backward_tan)
    if "tan_up" in waves:
        when_due(t - lag - stage, forward_tan)
    if "down" in waves:
        when_due(t - TURN - (2 * layers - 1 - stage), backward)
    if "up" in waves:
        when_due(t - stage, forward)
    if with_probes:
        group = pieces // 2 * rows
        for due, work in ((plan.ready_forward(t), ready_forward), (plan.ready_backward(t), ready_backward)):
            for layer, half in due:
                at = slice(half * group, (half + 1) * group)
                pl.when(stage == layer)(functools.partial(work, at))


def transposed(arrays):
    count = len(arrays)

    def kernel(*refs):
        for source, target in zip(refs[:count], refs[count:]):
            for c in range(0, source.shape[0], 256):
                target[:, c : c + 256] = source[c : c + 256, :].T

    return pl.pallas_call(
        kernel,
        out_shape=tuple(pltpu.VMEM(a.shape[::-1], a.dtype) for a in arrays),
        in_specs=[IN_VMEM] * count,
        out_specs=(IN_VMEM,) * count,
        compiler_params=pltpu.CompilerParams(vmem_limit_bytes=4 << 20),
        cost_estimate=pl.CostEstimate(flops=1 << 30, bytes_accessed=1 << 24, transcendentals=0),
        name="transposed",
    )(*[vmem(a) for a in arrays])


BATCHES = ((4,), (3, 5), (2, 6), (1, 7, 0))


def curvature_kernel(batches, sb_d, sb_f, *refs):
    mine, theirs = refs[: len(batches)], refs[len(batches) : 2 * len(batches)]
    hold = refs[-1]
    hidden = sb_f.shape[2]
    here = lax.axis_index("dp")
    chip, core = here // 2, lax.rem(here, 2)
    chips = lax.axis_size("dp") // 2
    step = hold.shape[0]
    part = step // 2
    for kept, given, batch in zip(mine, theirs, batches):
        for i, far in enumerate(batch):
            at = pl.ds(pl.multiple_of(lax.rem(chip + far, chips) * step, step), step)
            left = jnp.concatenate((sb_d[X, :, at], sb_d[TX, :, at]), axis=0)
            right = jnp.concatenate((sb_f[TP], sb_f[PR]), axis=0)
            hold[:, :hidden] = dot_first(left, right)
            left = jnp.concatenate((sb_d[TG, :, at], sb_d[G, :, at]), axis=0)
            right = jnp.concatenate((sb_f[A], sb_f[TA]), axis=0)
            hold[:, hidden:] = dot_first(left, right)
            kept[i] = hold[pl.ds(pl.multiple_of(core * part, part), part), :].astype(bf16)
            given[i] = hold[pl.ds(pl.multiple_of((1 - core) * part, part), part), :].astype(bf16)


def curvature(sb_d, sb_f, groups, batches):
    width, hidden = sb_d.shape[2], sb_f.shape[2]
    part = width // groups
    parts = tuple(pltpu.VMEM((len(batch), part, 2 * hidden), bf16) for batch in batches)
    outs = pl.pallas_call(
        functools.partial(curvature_kernel, batches),
        out_shape=parts + parts,
        in_specs=[IN_VMEM, IN_VMEM],
        out_specs=(IN_VMEM,) * (2 * len(batches)),
        scratch_shapes=[pltpu.VMEM((2 * part, 2 * hidden), f32)],
        compiler_params=pltpu.CompilerParams(vmem_limit_bytes=12 << 20),
        cost_estimate=pl.CostEstimate(flops=1 << 31, bytes_accessed=1 << 23, transcendentals=0),
        name="curvature",
    )(vmem(sb_d), vmem(sb_f))
    return outs[: len(batches)], outs[len(batches) :]


def routes(groups):
    return (
        [(i, (i + 2) % groups) for i in range(groups)],
        [(i, (i - 2) % groups) for i in range(groups)],
        [(i, i ^ 1) for i in range(groups)],
    )


def assemble(blocks, halves, groups, part, hidden):
    pieces = [(array, i, (i,), far, other) for array, far, other in blocks for i in range(2)]
    pieces += [(array, i, (), far, other) for array, i, far, other in halves]
    arrays = [b[0] for b in blocks] + [h[0] for h in halves]
    places = [p for p in range(len(blocks)) for _ in range(2)] + [len(blocks) + p for p in range(len(halves))]

    def kernel(*refs):
        sources, targets, sems = refs[: len(arrays)], refs[len(arrays) : -1], refs[-1]
        here = lax.axis_index("dp")
        chip, core = here // 2, lax.rem(here, 2)
        chips = groups // 2
        copies = []
        for n, ((_, probe, index, far, other), place) in enumerate(zip(pieces, places)):
            block = lax.rem(chip + far + chips, chips) * 2 + (1 - core if other else core)
            row = pl.ds(pl.multiple_of(block * part, part), part)
            source = sources[place].at[index] if index else sources[place]
            copies.append(pltpu.make_async_copy(source, targets[probe].at[row, :], sems.at[n]))
        for copy in copies:
            copy.start()
        for copy in copies:
            copy.wait()

    return pl.pallas_call(
        kernel,
        out_shape=tuple(pltpu.VMEM((groups * part, hidden), bf16) for _ in range(2)),
        in_specs=[ANYWHERE] * len(arrays),
        out_specs=(IN_VMEM,) * 2,
        scratch_shapes=[pltpu.SemaphoreType.DMA((len(pieces),))],
        compiler_params=pltpu.CompilerParams(vmem_limit_bytes=1 << 20),
        name="assemble",
    )(*arrays)


def scatter(mine, theirs, groups, hidden):
    ahead, behind, across = routes(groups)

    swapped = []

    def wide(kept, given):
        if swapped:
            given, swapped[-1] = lax.optimization_barrier((given, swapped[-1]))
        swapped.append(lax.ppermute(given, "dp", across))
        return kept.astype(f32) + swapped[-1].astype(f32)

    far = wide(mine[0], theirs[0])[0].astype(bf16)
    from_behind = lax.ppermute(far[:, :hidden], "dp", ahead)
    from_ahead = lax.ppermute(far[:, hidden:], "dp", behind)
    blank_half = ((0, 0), (0, hidden)), ((0, 0), (hidden, 0))
    pair = wide(mine[1], theirs[1])
    up = (pair[0] + jnp.pad(from_behind.astype(f32), blank_half[0])).astype(bf16)
    down = (pair[1] + jnp.pad(from_ahead.astype(f32), blank_half[1])).astype(bf16)
    for kept, given in zip(mine[2:], theirs[2:]):
        from_behind = lax.ppermute(up, "dp", ahead)
        from_ahead = lax.ppermute(down, "dp", behind)
        pair = wide(kept, given)
        up = (pair[0] + from_behind.astype(f32)).astype(bf16)
        down = (pair[1] + from_ahead.astype(f32)).astype(bf16)
    from_behind = lax.ppermute(up, "dp", ahead)
    from_ahead = lax.ppermute(down, "dp", behind)
    return pair[2] + from_behind.astype(f32) + from_ahead.astype(f32)


def on_device(embedded, targets, w_up, w_down, probe_up, probe_down):
    layers = lax.axis_size("pipe")
    groups = lax.axis_size("dp")
    tokens, width = embedded.shape
    hidden = w_up.shape[2]
    part = probe_up.shape[1]
    rows = tokens // PIECES
    loss_scale = 1.0 / (tokens * groups)
    plan = Plan(layers, PIECES, LAG)
    ahead, behind, across = routes(groups)

    swapped = []

    def swap(array):
        if swapped:
            array, swapped[-1] = lax.optimization_barrier((array, swapped[-1]))
        swapped.append(lax.ppermute(array, "dp", across))
        return swapped[-1]

    def ring(both):
        return [lax.ppermute(both[0], "dp", ahead), lax.ppermute(both[1], "dp", behind)]

    own = jnp.stack((probe_up[0], probe_down[0]))
    moving = ring([own, own])
    blocks = [(own, 0, False), (swap(own), 0, True)]
    halves = []

    weights, ends = [], load((w_up[0], w_down[0], embedded, targets))
    weights, ends = list(ends[:2]), list(ends[2:])
    turned = weights
    *state, nothing = blank(
        (
            ((4, tokens, width), bf16),
            ((4, tokens, hidden), bf16),
            ((6, tokens, width), f32),
            ((6, tokens, hidden), f32),
            ((3, tokens, 128), f32),
            ((rows, width), bf16),
        )
    )
    probes = None
    got = {"up": nothing}
    packet = pltpu.VMEM((rows, width), bf16)

    def keep(arrived, step):
        for array, away in zip(arrived, (-step, step)):
            blocks.extend([(array, away, False), (swap(array), away, True)])

    def part_of_tick(t, waves, with_probes, got, state):
        ways = [way for way in ("up", "down") if sends(waves, way)]
        operands = list(state) + weights + list(turned) + ends + (list(probes) if with_probes else [])
        operands += [got.get(name, nothing) for name in waves]
        outs = pl.pallas_call(
            functools.partial(tick_kernel, plan, t, waves, with_probes, loss_scale, rows, width, hidden),
            out_shape=tuple(pltpu.VMEM(s.shape, s.dtype) for s in state) + (packet,) * len(ways),
            in_specs=[IN_VMEM] * len(operands),
            out_specs=(IN_VMEM,) * (5 + len(ways)),
            input_output_aliases={i: i for i in range(5)},
            compiler_params=pltpu.CompilerParams(vmem_limit_bytes=8 << 20),
            cost_estimate=pl.CostEstimate(flops=1 << 30, bytes_accessed=1 << 23, transcendentals=0),
            name="tick",
        )(*[vmem(o) for o in operands])
        state, sent = outs[:5], dict(zip(ways, outs[5:]))
        arrived = {
            name: lax.ppermute(sent[name.removeprefix("tan_")], "pipe", edges)
            for name, edges in waves.items()
            if edges
        }
        return state, arrived

    for t in range(plan.ticks):
        waves = plan.waves(t)
        arrived = {}
        ready = bool(plan.ready_forward(t) or plan.ready_backward(t))
        following = {name: edges for name, edges in waves.items() if not name.startswith("tan_")}
        for name in ("tan_down", "tan_up"):
            if name in waves:
                state, more = part_of_tick(t, {name: waves[name]}, False, got, state)
                arrived.update(more)
        if following or ready:
            state, more = part_of_tick(t, following, ready, got, state)
            arrived.update(more)
        got = arrived
        if t <= 3:
            got["up"], *moving = lax.optimization_barrier((got["up"], *moving))
            moved = moving
            if t < 3:
                moving = ring(moved if t < 2 else [moved[0][0], moved[1][1]])
                keep(moved, t + 1)
            else:
                for i, array in enumerate(moved):
                    halves += [(array, i, 4, False), (swap(array), i, 4, True)]
                weights[0], got["up"] = lax.optimization_barrier((weights[0], got["up"]))
                turned = transposed(weights)
        if t == LAG - 2:
            probes = assemble(blocks, halves, groups, part, hidden)

    mine, theirs = (), ()
    for batches in (BATCHES[:1], BATCHES[1:]):
        kept, given = curvature(state[0], state[1], groups, batches)
        mine, theirs = mine + tuple(kept), theirs + tuple(given)
    summed = scatter(mine, theirs, groups, hidden)
    curv_up = probe_up[0].astype(f32) * summed[:, :hidden]
    curv_down = probe_down[0].astype(f32) * summed[:, hidden:]
    return (curv_up[None], curv_down[None])


def solution(mesh):
    in_specs = (
        P("dp", None),
        P("dp", None),
        P("pipe", None, None),
        P("pipe", None, None),
        P("pipe", "dp", None),
        P("pipe", "dp", None),
    )
    out_specs = (P("pipe", "dp", None), P("pipe", "dp", None))
    return jax.shard_map(
        on_device, mesh=mesh, in_specs=in_specs, out_specs=out_specs, check_vma=False
    )
```
